256 devices in a mesh: blk: 128 (over x, y, z_lo, core), uly: 2 (over z_hi).
Axes of the slice: x: 4, y: 4, z: 8 (z_hi: 2, z_lo: 4; z = z_hi * 4 + z_lo), core: 2. Of those that a mesh axis runs over, the one named last changes fastest.
Arguments:
- projected: bfloat16 [16384, 4, 512], P(('blk', 'uly')), may hold values from -6 to 6
- history: bfloat16 [16384, 1024], P(('blk', 'uly')), may hold values from -6 to 6
- buckets: int32 [16384], replicated, may hold values from 0 to 127, as said below
- time_table: float32 [8, 128], replicated, may hold values from -4 to 4
- out_weight: bfloat16 [512, 1024], replicated, may hold values from -0.25 to 0.25
- candidates: bfloat16 [16384, 8, 1024], P(('blk', 'uly')), may hold values from -6 to 6
- hidden_weight: bfloat16 [1024, 4096], replicated, may hold values from -0.1875 to 0.1875
- score_weight: float32 [4096], replicated, may hold values from -0.09375 to 0.09375
Outputs:
- layer_out: bfloat16 [16384, 1024], P(('blk', 'uly'))
- target_scores: float32 [16384, 8], P(('blk', 'uly'))
The draws below stay inside these ranges and needn't reach their ends.
Inputs may be any that keep to these rules, and one draw needn't show every extreme that they name: `buckets`: Non-decreasing along the history, 0 at the first event and 127 at the last, rising by 0 or 1 from one event to the next.
All inputs are finite; a program needn't handle non-finite values.
Results may differ from the reference program's by a relative error of at most 0.0066.
Values may be sent and summed in bfloat16 or wider, within the bound.
A program may use at most 192 MiB of HBM per device.

```python
import math
import jax
import jax.numpy as jnp
from jax import lax

D = 1024
HEADS = 8
DH = 64
HID = 4096
NB = 128
CANDS = 8
SEQ = 16384


def draw_buckets(key, part):
    key = jax.random.fold_in(key, 7)
    order = jax.random.permutation(key, SEQ - 1)
    marks = (order < NB - 1).astype(jnp.int32)
    rising = jnp.cumsum(marks, dtype=jnp.int32).astype(jnp.int32)
    return jnp.concatenate([jnp.zeros((1,), jnp.int32), rising])


def shard_levels(own_key, shape, split, least, top_value):
    gain, own = 1.0, jax.random.fold_in(own_key, 6)
    for position, blocks in split:
        steps = jnp.exp(jax.random.uniform(jax.random.fold_in(own, position), (blocks,), jnp.float32, least / len(split), top_value / len(split)))
        gain = gain * jnp.repeat(steps, shape[position] // blocks).reshape([-1 if axis == position else 1 for axis in range(len(shape))])
    return gain


def noise(key, dims, width, most, split=(), held_as=jnp.bfloat16):
    values = width * jax.random.normal(key, dims, jnp.float32)
    if split:
        values = values * shard_levels(key, dims, split, -0.22, 0.18)
    return jnp.clip(values, -most, most).astype(held_as)


def setup_inputs(seed: int = 0) -> dict:
    arg_keys = jax.random.split(jax.random.key(seed), 9)
    projected = noise(arg_keys[0], (SEQ, 4, HEADS * DH), 1.0, 6.0, ((0, 256),))
    history = noise(arg_keys[1], (SEQ, D), 1.0, 6.0, ((0, 256),))
    buckets = draw_buckets(jax.random.fold_in(arg_keys[8], 71), 0)
    time_table = noise(arg_keys[3], (HEADS, NB), 1.0, 4.0, (), jnp.float32)
    out_weight = noise(arg_keys[4], (HEADS * DH, D), (HEADS * DH) ** -0.5, 0.25)
    candidates = noise(arg_keys[5], (SEQ, CANDS, D), 1.0, 6.0, ((0, 256),))
    hidden_weight = noise(arg_keys[6], (D, HID), D ** -0.5, 0.1875)
    score_weight = noise(arg_keys[7], (HID,), HID ** -0.5, 0.09375, (), jnp.float32)
    return {"projected": projected, "history": history, "buckets": buckets, "time_table": time_table, "out_weight": out_weight, "candidates": candidates, "hidden_weight": hidden_weight, "score_weight": score_weight}


norm_eps = 1e-05

def reference(projected, history, buckets, time_table, out_weight, candidates, hidden_weight, score_weight):
    sequence = projected.shape[0]
    full_width = projected.shape[2]
    head_count = full_width // DH
    block_rows = math.gcd(sequence, 256)
    keys_all = projected[:, 3].astype(jnp.float32).reshape(sequence, head_count, DH)
    values_all = projected[:, 1].astype(jnp.float32).reshape(sequence, head_count, DH)
    key_pos = jnp.arange(sequence, dtype=jnp.int32)
    score_scale = DH ** (-0.5)

    def per_block(anchor):
        rows_in = lax.dynamic_slice_in_dim(projected, anchor, block_rows, 0)
        queries = rows_in[:, 2].astype(jnp.float32).reshape(block_rows, head_count, DH)
        row_pos = anchor + jnp.arange(block_rows, dtype=jnp.int32)
        row_buckets = lax.dynamic_slice_in_dim(buckets, anchor, block_rows, 0)
        distance = jnp.clip(row_buckets[:, None] - buckets[None, :], 0, NB - 1)
        bias = jnp.take(time_table, distance, axis=1)
        scores = jnp.einsum('qhd,khd->hqk', queries, keys_all) * score_scale + bias
        causal = row_pos[None, :, None] >= key_pos[None, None, :]
        weights = jnp.where(causal, jax.nn.silu(scores), 0.0).astype(jnp.bfloat16)
        attended = jnp.einsum('hqk,khd->qhd', weights.astype(jnp.float32), values_all)
        attended = attended.reshape(block_rows, full_width).astype(jnp.bfloat16)
        restored = attended.astype(jnp.float32)
        row_mean = lax.optimization_barrier(jnp.mean(restored, axis=-1, keepdims=True))
        centred = restored - row_mean
        row_var = lax.optimization_barrier(jnp.mean(centred * centred, axis=-1, keepdims=True))
        normed = centred * lax.rsqrt(row_var + norm_eps)
        gated = (normed * rows_in[:, 0].astype(jnp.float32)).astype(jnp.bfloat16)
        history_rows = lax.dynamic_slice_in_dim(history, anchor, block_rows, 0)
        layer_out = (jnp.dot(gated, out_weight, preferred_element_type=jnp.float32) + history_rows.astype(jnp.float32)).astype(jnp.bfloat16)
        cand_rows = lax.dynamic_slice_in_dim(candidates, anchor, block_rows, 0)
        paired = layer_out[:, None, :] * cand_rows
        hidden = jnp.dot(paired.reshape(block_rows * CANDS, -1), hidden_weight, preferred_element_type=jnp.float32)
        scored = lax.optimization_barrier(jnp.sum(jax.nn.silu(hidden) * score_weight, axis=-1)).reshape(block_rows, CANDS)
        return (layer_out, scored)
    anchors = jnp.arange(sequence // block_rows, dtype=jnp.int32) * block_rows
    layers, scored = lax.map(per_block, anchors)
    return (layers.reshape(sequence, -1), scored.reshape(sequence, CANDS))
```

```python
import functools

import jax
import jax.numpy as jnp
from jax import lax
from jax.experimental import pallas as pl
from jax.experimental.pallas import tpu as pltpu
from jax.sharding import PartitionSpec as P

MESH = pl.DeviceIdType.MESH
NORM_EPS = 1e-05
DH = 64
CANDS = 8
UNIT = 64
HEADS = 8
NB = 128
NT = (((1,), (1,)), ((), ()))


def device_at(x, y, z, core):
    return (x * 32 + y * 8 + lax.rem(z, 4) * 2 + core, z // 4)


def block_at(row, col):
    quarter = lax.rem(row + col, 4)
    return 4 * quarter + row + lax.rem(quarter, 2) * (3 - 2 * row)


def grid_of(x, y):
    row = y + lax.rem(x, 2) * (3 - 2 * y)
    return row, lax.rem(x - row + 4, 4)


def owner_of(row, col):
    x = lax.rem(row + col, 4)
    return x, row + lax.rem(x, 2) * (3 - 2 * row)


def worker_of(row, col):
    return col, lax.rem(row + 2, 4)


def hop(order):
    return jnp.where(order < 2, order, 5 - order)


def attention_kernel(
    kv_ref, q_ref, buckets_ref, table_ref, out_ref,
    kv, keys_hot, q_packed, q_wide, acc, outgoing, returned,
    p1_send, p1_recv, kv_send, kv_recv, q_send, q_recv, twin_send, twin_recv, back_send, back_recv,
):
    blk, uly = lax.axis_index("blk"), lax.axis_index("uly")
    x, y = blk // 32, lax.rem(blk // 8, 4)
    z_lo, core = lax.rem(blk // 2, 4), lax.rem(blk, 2)
    z = uly * 4 + z_lo
    home_row, home_col = grid_of(x, y)
    target_x, target_y = worker_of(home_row, home_col)
    col, row = x, lax.rem(y + 2, 4)
    source_x, source_y = owner_of(row, col)
    twin = device_at(x, y, z, 1 - core)

    def along_col(d):
        return device_at(x, lax.rem(y + d, 4), z, core)

    def along_row(d):
        return device_at(lax.rem(x + d, 4), y, z, core)

    barrier = pltpu.get_barrier_semaphore()

    def greet(i, _):
        pl.semaphore_signal(
            barrier, inc=1, device_id=device_at(source_x, source_y, i, core), device_id_type=MESH
        )
        return 0

    lax.fori_loop(0, 8, greet, 0)
    for d in range(1, 4):
        pl.semaphore_signal(barrier, inc=1, device_id=along_col(d), device_id_type=MESH)
        pl.semaphore_signal(barrier, inc=1, device_id=along_row(d), device_id_type=MESH)
    pl.semaphore_signal(barrier, inc=1, device_id=twin, device_id_type=MESH)
    pl.semaphore_wait(barrier, 15)

    def unit_offset(zz):
        return lax.rem(zz, 4) * 2 + zz // 4

    def phase1_kv(head, src_z):
        return pltpu.make_async_remote_copy(
            src_ref=kv_ref.at[head],
            dst_ref=kv.at[home_row, core, pl.ds(pl.multiple_of(unit_offset(src_z) * 64, 64), 64)],
            send_sem=p1_send.at[0, head],
            recv_sem=p1_recv.at[0, src_z],
            device_id=device_at(target_x, target_y, head, core),
            device_id_type=MESH,
        )

    def phase1_q(head, src_z):
        return pltpu.make_async_remote_copy(
            src_ref=q_ref.at[head],
            dst_ref=q_packed.at[home_col, pl.ds(pl.multiple_of(unit_offset(src_z) * 32, 32), 32)],
            send_sem=p1_send.at[1, head],
            recv_sem=p1_recv.at[1, src_z],
            device_id=device_at(target_x, target_y, head, core),
            device_id_type=MESH,
        )

    def arrived_kv(src_z):
        return pltpu.make_async_remote_copy(
            src_ref=kv_ref.at[0],
            dst_ref=kv.at[row, core, pl.ds(pl.multiple_of(unit_offset(src_z) * 64, 64), 64)],
            send_sem=p1_send.at[0, 0],
            recv_sem=p1_recv.at[0, src_z],
            device_id=device_at(source_x, source_y, src_z, core),
            device_id_type=MESH,
        )

    def arrived_q(src_z):
        return pltpu.make_async_remote_copy(
            src_ref=q_ref.at[0],
            dst_ref=q_packed.at[col, pl.ds(pl.multiple_of(unit_offset(src_z) * 32, 32), 32)],
            send_sem=p1_send.at[1, 0],
            recv_sem=p1_recv.at[1, src_z],
            device_id=device_at(source_x, source_y, src_z, core),
            device_id_type=MESH,
        )

    def send_first(d, _):
        phase1_kv(lax.rem(z + d, 8), z).start()
        return 0

    def send_second(d, _):
        phase1_q(lax.rem(z + d, 8), z).start()
        return 0

    lax.fori_loop(0, 8, send_first, 0)
    lax.fori_loop(0, 8, send_second, 0)

    lane = lax.broadcasted_iota(jnp.int32, (128, NB), 1)
    lane_f = lane.astype(jnp.float32)

    def bucket_columns(block):
        rows = buckets_ref[pl.ds(pl.multiple_of(block * 8, 8), 8), :]
        return jnp.transpose(rows.astype(jnp.float32))

    toeplitz = pltpu.roll(
        jnp.broadcast_to(table_ref[pl.ds(z, 1), :] * 0.5, (NB, NB)), 0, 1, stride=1, stride_axis=0
    ).astype(jnp.bfloat16)

    def key_columns(t, _):
        columns = bucket_columns(block_at(t, col))
        for stripe in range(8):
            hot = (columns[:, stripe : stripe + 1] == lane_f).astype(jnp.bfloat16)
            keys_hot[t, stripe % 2, (stripe // 2) * 128 : (stripe // 2 + 1) * 128, :] = hot
        return 0

    lax.fori_loop(0, 4, key_columns, 0)

    def query_columns(a, _):
        columns = bucket_columns(block_at(row, a))
        for stripe in range(4):
            own = jnp.where(
                core == 0, columns[:, 2 * stripe : 2 * stripe + 1], columns[:, 2 * stripe + 1 : 2 * stripe + 2]
            )
            hot = (own == lane_f).astype(jnp.bfloat16)
            bias = lax.dot_general(hot, toeplitz, NT, preferred_element_type=jnp.float32)
            q_wide[a, stripe * 128 : (stripe + 1) * 128, NB:] = bias.astype(jnp.bfloat16)
        acc[a] = jnp.zeros((512, 128), jnp.float32)
        return 0

    lax.fori_loop(0, 4, query_columns, 0)

    def unpack_queries(a):
        packed = q_packed[a].astype(jnp.float32).reshape(8, 32, 128)
        low = lax.broadcasted_iota(jnp.int32, (8, 32, 128), 2) < DH
        first = jnp.where(low, packed, 0.0)
        second = jnp.where(low, pltpu.roll(packed, DH, 2), 0.0)
        q_wide[a, :, :NB] = (
            jnp.concatenate([first, second], axis=1).reshape(512, 128).astype(jnp.bfloat16)
        )

    def kv_copy(slot, d):
        return pltpu.make_async_remote_copy(
            src_ref=kv.at[slot, core],
            dst_ref=kv.at[slot, core],
            send_sem=kv_send.at[d - 1],
            recv_sem=kv_recv.at[d - 1],
            device_id=along_col(d),
            device_id_type=MESH,
        )

    def q_copy(slot, d):
        return pltpu.make_async_remote_copy(
            src_ref=q_packed.at[slot],
            dst_ref=q_packed.at[slot],
            send_sem=q_send.at[d - 1],
            recv_sem=q_recv.at[d - 1],
            device_id=along_row(d),
            device_id_type=MESH,
        )

    def twin_copy(slot, half, d):
        return pltpu.make_async_remote_copy(
            src_ref=kv.at[slot, half],
            dst_ref=kv.at[slot, half],
            send_sem=twin_send.at[d],
            recv_sem=twin_recv.at[d],
            device_id=twin,
            device_id_type=MESH,
        )

    def wait_kv(i, _):
        arrived_kv(i).wait_recv()
        return 0

    def wait_q(i, _):
        arrived_q(i).wait_recv()
        return 0

    lax.fori_loop(0, 8, wait_kv, 0)
    for d in (1, 3, 2):
        kv_copy(row, d).start()
    twin_copy(row, core, 0).start()
    lax.fori_loop(0, 8, wait_q, 0)
    for d in (1, 3, 2):
        q_copy(col, d).start()
    unpack_queries(col)

    def activate(halved):
        return (halved + halved * jnp.tanh(halved)).astype(jnp.bfloat16)

    def attend_diagonal(half):
        held = kv[row, half]
        wide = jnp.concatenate([held, keys_hot[row, half]], axis=1)
        scores = lax.dot_general(q_wide[col], wide, NT, preferred_element_type=jnp.float32)
        place_q = lax.broadcasted_iota(jnp.int32, (512, 512), 0)
        place_k = lax.broadcasted_iota(jnp.int32, (512, 512), 1)
        event_q = place_q + (place_q // 128) * 128 + core * 128
        event_k = place_k + (place_k // 128) * 128 + half * 128
        weights = jnp.where(event_k <= event_q, activate(scores), jnp.zeros((), jnp.bfloat16))
        acc[col] += jnp.dot(weights, held, preferred_element_type=jnp.float32)

    def attend(a, t):
        @pl.when(block_at(t, col) < block_at(row, a))
        def _():
            held = kv[t].reshape(1024, 128)
            wide = jnp.concatenate([held, keys_hot[t].reshape(1024, 128)], axis=1)
            scores = lax.dot_general(q_wide[a], wide, NT, preferred_element_type=jnp.float32)
            acc[a] += jnp.dot(activate(scores), held, preferred_element_type=jnp.float32)

    def query_member(n):
        return lax.rem(col - hop(n) + 4, 4)

    def key_member(n):
        return lax.rem(row - hop(n) + 4, 4)

    attend_diagonal(core)
    twin_copy(row, 1 - core, 0).wait_recv()
    attend_diagonal(1 - core)

    def arrive(d):
        t = lax.rem(row - d + 4, 4)
        a = lax.rem(col - d + 4, 4)
        kv_copy(t, d).wait_recv()
        twin_copy(t, core, d).start()
        q_copy(a, d).wait_recv()
        unpack_queries(a)
        twin_copy(t, 1 - core, d).wait_recv()

    for n, d in ((1, 1), (2, 3)):
        arrive(d)

        def pair(k, _, n=n):
            newest = k <= n
            attend(
                query_member(jnp.where(newest, n, k - n - 1)),
                key_member(jnp.where(newest, k, n)),
            )
            return 0

        lax.fori_loop(0, 2 * n + 1, pair, 0)

    arrive(2)

    low32 = lax.broadcasted_iota(jnp.int32, (8, 32, 128), 2) < DH

    def back_copy(a, unit):
        owner_x, owner_y = owner_of(row, a)
        owner_z = lax.rem(unit, 2) * 4 + unit // 2
        return pltpu.make_async_remote_copy(
            src_ref=outgoing.at[a, unit],
            dst_ref=returned.at[z, col],
            send_sem=back_send.at[a, unit],
            recv_sem=back_recv.at[z, col],
            device_id=device_at(owner_x, owner_y, owner_z, core),
            device_id_type=MESH,
        )

    def finish(n, _):
        a = query_member(n)

        def last_pair(m, _):
            attend(a, key_member(m))
            return 0

        lax.fori_loop(jnp.where(n < 3, 3, 0), 4, last_pair, 0)
        total = acc[a].reshape(8, 64, 128)
        outgoing[a] = jnp.where(low32, pltpu.roll(total[:, :32], DH, 2), total[:, 32:]).astype(jnp.bfloat16)

        def send_back(unit, _):
            back_copy(a, unit).start()
            return 0

        lax.fori_loop(0, 8, send_back, 0)
        return 0

    lax.fori_loop(0, 4, finish, 0)

    def sent_first(i, _):
        phase1_kv(i, z).wait_send()
        phase1_q(i, z).wait_send()
        return 0

    lax.fori_loop(0, 8, sent_first, 0)
    twin_copy(row, core, 0).wait_send()
    for d in range(1, 4):
        kv_copy(row, d).wait_send()
        q_copy(col, d).wait_send()
        twin_copy(lax.rem(row - d + 4, 4), core, d).wait_send()

    def sent_back(i, _):
        back_copy(i // 8, lax.rem(i, 8)).wait_send()
        return 0

    lax.fori_loop(0, 32, sent_back, 0)

    def got_back(i, _):
        head, part = i // 4, lax.rem(i, 4)
        pltpu.make_async_remote_copy(
            src_ref=outgoing.at[0, 0],
            dst_ref=returned.at[head, part],
            send_sem=back_send.at[0, 0],
            recv_sem=back_recv.at[head, part],
            device_id=device_at(target_x, target_y, head, core),
            device_id_type=MESH,
        ).wait_recv()
        return 0

    lax.fori_loop(0, 32, got_back, 0)
    low = lax.broadcasted_iota(jnp.int32, (32, 128), 1) < DH
    sums = [jnp.sum(returned[h].astype(jnp.float32), axis=0) for h in range(HEADS)]
    for pair_at in range(HEADS // 2):
        even, odd = sums[2 * pair_at], sums[2 * pair_at + 1]
        lanes = slice(pair_at * 128, pair_at * 128 + 128)
        out_ref[:32, lanes] = jnp.where(low, even, pltpu.roll(odd, DH, 1)).astype(jnp.bfloat16)
        out_ref[32:, lanes] = jnp.where(low, pltpu.roll(even, DH, 1), odd).astype(jnp.bfloat16)


def dense_kernel(
    attended_ref, gate_ref, out_weight_ref, history_ref, candidates_ref, hidden_ref, score_ref,
    layer_ref, scores_ref, paired, acc,
):
    step = pl.program_id(0)

    @pl.when(step == 0)
    def _():
        restored = attended_ref[...].astype(jnp.float32)
        centred = restored - jnp.mean(restored, axis=-1, keepdims=True)
        variance = jnp.mean(centred * centred, axis=-1, keepdims=True)
        normed = centred * lax.rsqrt(variance + NORM_EPS)
        gated = (normed * gate_ref[...].astype(jnp.float32)).astype(jnp.bfloat16)
        layer = jnp.dot(gated, out_weight_ref[...], preferred_element_type=jnp.float32)
        layer = (layer + history_ref[...].astype(jnp.float32)).astype(jnp.bfloat16)
        layer_ref[...] = layer
        halved = layer.astype(jnp.float32) * 0.5
        for part in range(4):
            events = halved[part * 16 : part * 16 + 16]
            rows = slice(part * 128, part * 128 + 128)
            spread = jnp.broadcast_to(events[:, None, :], (16, CANDS, events.shape[1])).reshape(128, -1)
            paired[rows] = (spread * candidates_ref[rows].astype(jnp.float32)).astype(jnp.bfloat16)
        acc[...] = jnp.zeros_like(acc)

    halved = jnp.dot(paired[...], hidden_ref[...], preferred_element_type=jnp.float32)
    scored = (halved + halved * jnp.tanh(halved)) * score_ref[...]
    total = acc[...]
    for part in range(scored.shape[1] // 128):
        total += scored[:, part * 128 : part * 128 + 128]
    acc[...] = total

    @pl.when(step == pl.num_programs(0) - 1)
    def _():
        scores_ref[...] = jnp.sum(acc[...].reshape(UNIT, CANDS, 128), axis=-1)


def per_device(
    projected, history, buckets, time_table, out_weight, candidates, hidden_weight, score_weight
):
    width = projected.shape[2]
    dim = history.shape[1]
    hid = hidden_weight.shape[1]
    heads = projected.reshape(UNIT, 4, HEADS, DH)
    kv_send = jnp.concatenate([heads[:, 3], heads[:, 1]], axis=-1).transpose(1, 0, 2)
    q_send = (heads[:, 2] * jnp.bfloat16(0.0625)).reshape(2, 32, HEADS, DH)
    q_send = q_send.transpose(2, 1, 0, 3).reshape(HEADS, 32, 2 * DH)
    vmem = pl.BlockSpec(memory_space=pltpu.VMEM)
    dma = pltpu.SemaphoreType.DMA
    attended = pl.pallas_call(
        attention_kernel,
        out_shape=jax.ShapeDtypeStruct((UNIT, width), jnp.bfloat16),
        in_specs=[vmem] * 4,
        out_specs=vmem,
        scratch_shapes=[
            pltpu.VMEM((4, 2, 512, 128), jnp.bfloat16),
            pltpu.VMEM((4, 2, 512, 128), jnp.bfloat16),
            pltpu.VMEM((4, 256, 128), jnp.bfloat16),
            pltpu.VMEM((4, 512, 256), jnp.bfloat16),
            pltpu.VMEM((4, 512, 128), jnp.float32),
            pltpu.VMEM((4, 8, 32, 128), jnp.bfloat16),
            pltpu.VMEM((8, 4, 32, 128), jnp.bfloat16),
            dma((2, 8)), dma((2, 8)), dma((3,)), dma((3,)), dma((3,)), dma((3,)),
            dma((4,)), dma((4,)), dma((4, 8)), dma((8, 4)),
        ],
        compiler_params=pltpu.CompilerParams(
            collective_id=0, has_side_effects=True, vmem_limit_bytes=32 << 20
        ),
        name="attend",
    )(kv_send, q_send, buckets.reshape(128, 128), time_table)

    tile = 512
    whole = lambda shape: pl.BlockSpec(shape, lambda i: (0,) * len(shape))
    layer, scores = pl.pallas_call(
        dense_kernel,
        grid=(hid // tile,),
        out_shape=(
            jax.ShapeDtypeStruct((UNIT, dim), jnp.bfloat16),
            jax.ShapeDtypeStruct((UNIT, CANDS), jnp.float32),
        ),
        in_specs=[
            whole((UNIT, width)),
            whole((UNIT, width)),
            whole((width, dim)),
            whole((UNIT, dim)),
            whole((UNIT * CANDS, dim)),
            pl.BlockSpec((dim, tile), lambda i: (0, i)),
            pl.BlockSpec((1, tile), lambda i: (0, i)),
        ],
        out_specs=(whole((UNIT, dim)), whole((UNIT, CANDS))),
        scratch_shapes=[
            pltpu.VMEM((UNIT * CANDS, dim), jnp.bfloat16),
            pltpu.VMEM((UNIT * CANDS, 128), jnp.float32),
        ],
        compiler_params=pltpu.CompilerParams(vmem_limit_bytes=32 << 20),
        name="score",
    )(
        attended, projected[:, 0], out_weight, history,
        candidates.reshape(UNIT * CANDS, dim), hidden_weight, score_weight.reshape(1, hid),
    )
    return layer, scores


def solution(mesh):
    rows = ("blk", "uly")
    return jax.shard_map(
        per_device,
        mesh=mesh,
        in_specs=(
            P(rows, None, None), P(rows, None), P(), P(), P(), P(rows, None, None), P(), P(),
        ),
        out_specs=(P(rows, None), P(rows, None)),
        check_vma=False,
    )
```

```python
import jax
import jax.numpy as jnp
from jax import lax
from jax.experimental import pallas as pl
from jax.experimental.pallas import tpu as pltpu
from jax.sharding import PartitionSpec as P

MESH = pl.DeviceIdType.MESH
NORM_EPS = 1e-05
DH = 64
CANDS = 8
UNIT = 64
HEADS = 8
HID_TILE = 1024
NB = 128
NT = (((1,), (1,)), ((), ()))


def device_at(x, y, z, core):
    return (x * 32 + y * 8 + lax.rem(z, 4) * 2 + core, z // 4)


def mirrored(row, col):
    return col + lax.rem(row, 2) * (3 - 2 * col)


def block_at(row, col):
    return 4 * mirrored(row, col) + row


def hop(order):
    return jnp.where(order < 2, order, 5 - order)


def layer_kernel(
    projected_hbm, buckets_hbm, table_hbm, out_weight_hbm, history_hbm, candidates_hbm, hidden_hbm, score_hbm,
    layer_ref, scores_ref,
    projected, buckets_ref, table_ref, out_weight, history, candidates, hidden_weight, score_weight, load_sem,
    planes, kv_ref, q_ref, paired, score_acc,
    kv, keys_hot, q_packed, q_wide, acc, outgoing, returned,
    p1_send, p1_recv, kv_send, kv_recv, q_send, q_recv, twin_send, twin_recv, back_send, back_recv,
):
    blk, uly = lax.axis_index("blk"), lax.axis_index("uly")
    x, y = blk // 32, lax.rem(blk // 8, 4)
    z_lo, core = lax.rem(blk // 2, 4), lax.rem(blk, 2)
    z = uly * 4 + z_lo
    home_row, home_col = y, mirrored(y, x)
    target_x, target_y = home_col, home_row
    stays = y % 2 == 0
    row, col = y, x
    source_x, source_y = mirrored(row, col), row
    twin = device_at(x, y, z, 1 - core)

    def along_col(d):
        return device_at(x, lax.rem(y + d, 4), z, core)

    def along_row(d):
        return device_at(lax.rem(x + d, 4), y, z, core)

    loads = [
        pltpu.make_async_copy(src, dst, load_sem.at[i])
        for i, (src, dst) in enumerate(
            (
                (projected_hbm, projected),
                (buckets_hbm, buckets_ref),
                (table_hbm, table_ref),
                (out_weight_hbm, out_weight),
                (history_hbm, history),
                (candidates_hbm, candidates),
                (score_hbm, score_weight),
                (hidden_hbm, hidden_weight),
            )
        )
    ]
    for load in loads[:3]:
        load.start()

    barrier = pltpu.get_barrier_semaphore()

    def greet(i, _):
        @pl.when(jnp.logical_not(jnp.logical_and(stays, i == z)))
        def _():
            pl.semaphore_signal(
                barrier, inc=1, device_id=device_at(source_x, source_y, i, core), device_id_type=MESH
            )

        return 0

    lax.fori_loop(0, 8, greet, 0)
    for d in range(1, 4):
        pl.semaphore_signal(barrier, inc=1, device_id=along_col(d), device_id_type=MESH)
        pl.semaphore_signal(barrier, inc=1, device_id=along_row(d), device_id_type=MESH)
    pl.semaphore_signal(barrier, inc=1, device_id=twin, device_id_type=MESH)

    low64 = lax.broadcasted_iota(jnp.int32, (UNIT, 128), 1) < DH
    low_half = lax.broadcasted_iota(jnp.int32, (UNIT // 2, 128), 1) < DH
    loads[0].wait()
    for group in range(HEADS // 2):
        lanes = slice(group * 128, group * 128 + 128)
        planes[group] = projected[:, :, lanes].astype(jnp.float32).reshape(UNIT * 4, 128)
        value, query, key = [planes[group, pl.ds(plane, UNIT, stride=4), :] for plane in (1, 2, 3)]
        kv_ref[2 * group] = jnp.where(low64, key, pltpu.roll(value, DH, 1)).astype(jnp.bfloat16)
        kv_ref[2 * group + 1] = jnp.where(low64, pltpu.roll(key, DH, 1), value).astype(jnp.bfloat16)
        early, late = query[:32] * 0.0625, query[32:] * 0.0625
        q_ref[2 * group] = jnp.where(low_half, early, pltpu.roll(late, DH, 1)).astype(jnp.bfloat16)
        q_ref[2 * group + 1] = jnp.where(low_half, pltpu.roll(early, DH, 1), late).astype(jnp.bfloat16)
    pl.semaphore_wait(barrier, 14 + lax.rem(y, 2))

    def unit_offset(zz):
        return lax.rem(zz, 4) * 2 + zz // 4

    def phase1_kv(head, src_z):
        return pltpu.make_async_remote_copy(
            src_ref=kv_ref.at[head],
            dst_ref=kv.at[home_row, core, pl.ds(pl.multiple_of(unit_offset(src_z) * 64, 64), 64)],
            send_sem=p1_send.at[0, head],
            recv_sem=p1_recv.at[0, src_z],
            device_id=device_at(target_x, target_y, head, core),
            device_id_type=MESH,
        )

    def phase1_q(head, src_z):
        return pltpu.make_async_remote_copy(
            src_ref=q_ref.at[head],
            dst_ref=q_packed.at[home_col, pl.ds(pl.multiple_of(unit_offset(src_z) * 32, 32), 32)],
            send_sem=p1_send.at[1, head],
            recv_sem=p1_recv.at[1, src_z],
            device_id=device_at(target_x, target_y, head, core),
            device_id_type=MESH,
        )

    def arrived_kv(src_z):
        return pltpu.make_async_remote_copy(
            src_ref=kv_ref.at[0],
            dst_ref=kv.at[row, core, pl.ds(pl.multiple_of(unit_offset(src_z) * 64, 64), 64)],
            send_sem=p1_send.at[0, 0],
            recv_sem=p1_recv.at[0, src_z],
            device_id=device_at(source_x, source_y, src_z, core),
            device_id_type=MESH,
        )

    def arrived_q(src_z):
        return pltpu.make_async_remote_copy(
            src_ref=q_ref.at[0],
            dst_ref=q_packed.at[col, pl.ds(pl.multiple_of(unit_offset(src_z) * 32, 32), 32)],
            send_sem=p1_send.at[1, 0],
            recv_sem=p1_recv.at[1, src_z],
            device_id=device_at(source_x, source_y, src_z, core),
            device_id_type=MESH,
        )

    def away(i):
        return lax.rem((i + 1) // 2 + lax.rem(i + 1, 2) * (8 - 2 * ((i + 1) // 2)) + 8, 8)

    def start_either(here, local, remote):
        @pl.when(here)
        def _():
            pltpu.make_async_copy(*local).start()

        @pl.when(jnp.logical_not(here))
        def _():
            remote().start()

    def send_first(i, _):
        head = lax.rem(z + away(i), 8)
        place = kv.at[home_row, core, pl.ds(pl.multiple_of(unit_offset(z) * 64, 64), 64)]
        start_either(
            jnp.logical_and(stays, head == z),
            (kv_ref.at[head], place, p1_recv.at[0, z]),
            lambda: phase1_kv(head, z),
        )
        return 0

    def send_second(i, _):
        head = lax.rem(z + away(i), 8)
        place = q_packed.at[home_col, pl.ds(pl.multiple_of(unit_offset(z) * 32, 32), 32)]
        start_either(
            jnp.logical_and(stays, head == z),
            (q_ref.at[head], place, p1_recv.at[1, z]),
            lambda: phase1_q(head, z),
        )
        return 0

    lax.fori_loop(0, 8, send_first, 0)
    lax.fori_loop(0, 8, send_second, 0)
    for load in loads[3:]:
        load.start()
    for load in loads[1:3]:
        load.wait()

    lane = lax.broadcasted_iota(jnp.int32, (128, NB), 1)
    lane_f = lane.astype(jnp.float32)

    def bucket_columns(block):
        rows = buckets_ref[pl.ds(pl.multiple_of(block * 8, 8), 8), :]
        return jnp.transpose(rows.astype(jnp.float32))

    toeplitz = pltpu.roll(
        jnp.broadcast_to(table_ref[pl.ds(z, 1), :] * 0.5, (NB, NB)), 0, 1, stride=1, stride_axis=0
    ).astype(jnp.bfloat16)

    def key_columns(t, _):
        columns = bucket_columns(block_at(t, col))
        for stripe in range(8):
            hot = (columns[:, stripe : stripe + 1] == lane_f).astype(jnp.bfloat16)
            keys_hot[t, stripe % 2, (stripe // 2) * 128 : (stripe // 2 + 1) * 128, :] = hot
        return 0

    lax.fori_loop(0, 4, key_columns, 0)

    def query_columns(a, _):
        columns = bucket_columns(block_at(row, a))
        for stripe in range(4):
            own = jnp.where(
                core == 0, columns[:, 2 * stripe : 2 * stripe + 1], columns[:, 2 * stripe + 1 : 2 * stripe + 2]
            )
            hot = (own == lane_f).astype(jnp.bfloat16)
            bias = lax.dot_general(hot, toeplitz, NT, preferred_element_type=jnp.float32)
            q_wide[a, stripe * 128 : (stripe + 1) * 128, NB:] = bias.astype(jnp.bfloat16)
        acc[a] = jnp.zeros((512, 128), jnp.float32)
        return 0

    lax.fori_loop(0, 4, query_columns, 0)

    def unpack_queries(a):
        packed = q_packed[a].astype(jnp.float32).reshape(8, 32, 128)
        low = lax.broadcasted_iota(jnp.int32, (8, 32, 128), 2) < DH
        first = jnp.where(low, packed, 0.0)
        second = jnp.where(low, pltpu.roll(packed, DH, 2), 0.0)
        q_wide[a, :, :NB] = (
            jnp.concatenate([first, second], axis=1).reshape(512, 128).astype(jnp.bfloat16)
        )

    def kv_copy(slot, d):
        return pltpu.make_async_remote_copy(
            src_ref=kv.at[slot, core],
            dst_ref=kv.at[slot, core],
            send_sem=kv_send.at[d - 1],
            recv_sem=kv_recv.at[d - 1],
            device_id=along_col(d),
            device_id_type=MESH,
        )

    def q_copy(slot, d):
        return pltpu.make_async_remote_copy(
            src_ref=q_packed.at[slot],
            dst_ref=q_packed.at[slot],
            send_sem=q_send.at[d - 1],
            recv_sem=q_recv.at[d - 1],
            device_id=along_row(d),
            device_id_type=MESH,
        )

    def twin_copy(slot, half, d):
        return pltpu.make_async_remote_copy(
            src_ref=kv.at[slot, half],
            dst_ref=kv.at[slot, half],
            send_sem=twin_send.at[d],
            recv_sem=twin_recv.at[d],
            device_id=twin,
            device_id_type=MESH,
        )

    def forward(i, _):
        source = lax.rem(z + 8 - away(i), 8)
        arrived_kv(source).wait_recv()
        piece = kv.at[row, core, pl.ds(pl.multiple_of(unit_offset(source) * 64, 64), 64)]
        for d in (1, 3):
            pltpu.make_async_remote_copy(
                src_ref=piece, dst_ref=piece, send_sem=kv_send.at[d - 1], recv_sem=kv_recv.at[d - 1],
                device_id=along_col(d), device_id_type=MESH,
            ).start()
        pltpu.make_async_remote_copy(
            src_ref=piece, dst_ref=piece, send_sem=twin_send.at[0], recv_sem=twin_recv.at[0],
            device_id=twin, device_id_type=MESH,
        ).start()
        return 0

    def wait_q(i, _):
        arrived_q(i).wait_recv()
        return 0

    lax.fori_loop(0, 8, forward, 0)
    kv_copy(row, 2).start()
    lax.fori_loop(0, 8, wait_q, 0)
    for d in (1, 3, 2):
        q_copy(col, d).start()
    unpack_queries(col)

    def activate(halved):
        return (halved + halved * jnp.tanh(halved)).astype(jnp.bfloat16)

    def attend_diagonal(half):
        held = kv[row, half]
        wide = jnp.concatenate([held, keys_hot[row, half]], axis=1)
        scores = lax.dot_general(q_wide[col], wide, NT, preferred_element_type=jnp.float32)
        place_q = lax.broadcasted_iota(jnp.int32, (512, 512), 0)
        place_k = lax.broadcasted_iota(jnp.int32, (512, 512), 1)
        event_q = place_q + (place_q // 128) * 128 + core * 128
        event_k = place_k + (place_k // 128) * 128 + half * 128
        weights = jnp.where(event_k <= event_q, activate(scores), jnp.zeros((), jnp.bfloat16))
        acc[col] += jnp.dot(weights, held, preferred_element_type=jnp.float32)

    def attend(a, t):
        @pl.when(block_at(t, col) < block_at(row, a))
        def _():
            held = kv[t].reshape(1024, 128)
            wide = jnp.concatenate([held, keys_hot[t].reshape(1024, 128)], axis=1)
            scores = lax.dot_general(q_wide[a], wide, NT, preferred_element_type=jnp.float32)
            acc[a] += jnp.dot(activate(scores), held, preferred_element_type=jnp.float32)

    def query_member(n):
        return lax.rem(col - hop(n) + 4, 4)

    def key_member(n):
        return lax.rem(row - hop(n) + 4, 4)

    attend_diagonal(core)
    twin_copy(row, 1 - core, 0).wait_recv()
    attend_diagonal(1 - core)

    def pass_on(d):
        t = lax.rem(row - d + 4, 4)
        kv_copy(t, d).wait_recv()
        twin_copy(t, core, d).start()

    def take_queries(d):
        a = lax.rem(col - d + 4, 4)
        q_copy(a, d).wait_recv()
        unpack_queries(a)

    def take_keys(d):
        twin_copy(lax.rem(row - d + 4, 4), 1 - core, d).wait_recv()

    def attend_stage(n):
        def pair(k, _):
            newest = k <= n
            attend(
                query_member(jnp.where(newest, n, k - n - 1)),
                key_member(jnp.where(newest, k, n)),
            )
            return 0

        lax.fori_loop(0, 2 * n + 1, pair, 0)

    pass_on(1)
    pass_on(3)
    take_queries(1)
    take_keys(1)
    attend_stage(1)
    take_queries(3)
    take_keys(3)
    pass_on(2)
    attend_stage(2)
    take_queries(2)

    def last_queries(m, _):
        attend(query_member(3), key_member(m))
        return 0

    lax.fori_loop(0, 3, last_queries, 0)
    take_keys(2)

    low32 = lax.broadcasted_iota(jnp.int32, (8, 32, 128), 2) < DH

    def stays_back(a, unit):
        return jnp.logical_and(mirrored(row, a) == x, unit == unit_offset(z))

    def back_copy(a, unit):
        owner_x, owner_y = mirrored(row, a), row
        owner_z = lax.rem(unit, 2) * 4 + unit // 2
        return pltpu.make_async_remote_copy(
            src_ref=outgoing.at[a, unit],
            dst_ref=returned.at[z, col],
            send_sem=back_send.at[a, unit],
            recv_sem=back_recv.at[z, col],
            device_id=device_at(owner_x, owner_y, owner_z, core),
            device_id_type=MESH,
        )

    def finish(n, _):
        a = query_member(n)

        attend(a, key_member(3))
        total = acc[a].reshape(8, 64, 128)
        outgoing[a] = jnp.where(low32, pltpu.roll(total[:, :32], DH, 2), total[:, 32:]).astype(jnp.bfloat16)

        def send_back(unit, _):
            start_either(
                stays_back(a, unit),
                (outgoing.at[a, unit], returned.at[z, col], back_recv.at[z, col]),
                lambda: back_copy(a, unit),
            )
            return 0

        lax.fori_loop(0, 8, send_back, 0)
        return 0

    lax.fori_loop(0, 4, finish, 0)

    def sent_first(i, _):
        @pl.when(jnp.logical_not(jnp.logical_and(stays, i == z)))
        def _():
            phase1_kv(i, z).wait_send()
            phase1_q(i, z).wait_send()

        return 0

    lax.fori_loop(0, 8, sent_first, 0)
    twin_copy(row, core, 0).wait_send()
    for d in range(1, 4):
        kv_copy(row, d).wait_send()
        q_copy(col, d).wait_send()
        twin_copy(lax.rem(row - d + 4, 4), core, d).wait_send()

    def sent_back(i, _):
        a, unit = i // 8, lax.rem(i, 8)

        @pl.when(jnp.logical_not(stays_back(a, unit)))
        def _():
            back_copy(a, unit).wait_send()

        return 0

    lax.fori_loop(0, 32, sent_back, 0)

    def got_back(i, _):
        head, part = i // 4, lax.rem(i, 4)
        pltpu.make_async_remote_copy(
            src_ref=outgoing.at[0, 0],
            dst_ref=returned.at[head, part],
            send_sem=back_send.at[0, 0],
            recv_sem=back_recv.at[head, part],
            device_id=device_at(target_x, target_y, head, core),
            device_id_type=MESH,
        ).wait_recv()
        return 0

    lax.fori_loop(0, 32, got_back, 0)
    sums = [
        jnp.sum(returned[h].astype(jnp.float32), axis=0).astype(jnp.bfloat16).astype(jnp.float32)
        for h in range(HEADS)
    ]
    parts = []
    for group in range(HEADS // 2):
        even, odd = sums[2 * group], sums[2 * group + 1]
        first = jnp.where(low_half, even, pltpu.roll(odd, DH, 1))
        second = jnp.where(low_half, pltpu.roll(even, DH, 1), odd)
        parts.append(jnp.concatenate([first, second], axis=0))
    restored = jnp.concatenate(parts, axis=1)

    centred = restored - jnp.mean(restored, axis=-1, keepdims=True)
    variance = jnp.mean(centred * centred, axis=-1, keepdims=True)
    normed = centred * lax.rsqrt(variance + NORM_EPS)
    gate = jnp.concatenate([planes[group, pl.ds(0, UNIT, stride=4), :] for group in range(HEADS // 2)], axis=1)
    gated = (normed * gate).astype(jnp.bfloat16)
    for load in loads[3:]:
        load.wait()
    layer = jnp.dot(gated, out_weight[...], preferred_element_type=jnp.float32)
    layer = (layer + history[...].astype(jnp.float32)).astype(jnp.bfloat16)
    layer_ref[...] = layer
    halved_layer = layer.astype(jnp.float32) * 0.5
    for part in range(4):
        events = halved_layer[part * 16 : part * 16 + 16]
        rows = slice(part * 128, part * 128 + 128)
        spread = jnp.broadcast_to(events[:, None, :], (16, CANDS, events.shape[1])).reshape(128, -1)
        paired[rows] = (spread * candidates[rows].astype(jnp.float32)).astype(jnp.bfloat16)
    score_acc[...] = jnp.zeros_like(score_acc)

    def score_tile(i, _):
        columns = pl.ds(pl.multiple_of(i * HID_TILE, HID_TILE), HID_TILE)
        halved = jnp.dot(paired[...], hidden_weight[:, columns], preferred_element_type=jnp.float32)
        scored = (halved + halved * jnp.tanh(halved)) * score_weight[:, columns]
        total = score_acc[...]
        for part in range(HID_TILE // 128):
            total += scored[:, part * 128 : part * 128 + 128]
        score_acc[...] = total
        return 0

    lax.fori_loop(0, hidden_weight.shape[1] // HID_TILE, score_tile, 0)
    scores_ref[...] = jnp.transpose(jnp.sum(score_acc[...].reshape(UNIT, CANDS, 128), axis=-1))


def per_device(
    projected, history, buckets, time_table, out_weight, candidates, hidden_weight, score_weight
):
    width = projected.shape[2]
    dim = history.shape[1]
    hid = hidden_weight.shape[1]
    vmem = pl.BlockSpec(memory_space=pltpu.VMEM)
    hbm = pl.BlockSpec(memory_space=pl.ANY)
    dma = pltpu.SemaphoreType.DMA
    bf16, f32 = jnp.bfloat16, jnp.float32
    rows = UNIT * CANDS
    layer, scores = pl.pallas_call(
        layer_kernel,
        out_shape=(
            jax.ShapeDtypeStruct((UNIT, dim), bf16),
            jax.ShapeDtypeStruct((CANDS, UNIT), f32),
        ),
        in_specs=[hbm] * 8,
        out_specs=(vmem, vmem),
        scratch_shapes=[
            pltpu.VMEM((UNIT, 4, width), bf16),
            pltpu.VMEM((128, 128), jnp.int32),
            pltpu.VMEM((HEADS, NB), f32),
            pltpu.VMEM((width, dim), bf16),
            pltpu.VMEM((UNIT, dim), bf16),
            pltpu.VMEM((rows, dim), bf16),
            pltpu.VMEM((dim, hid), bf16),
            pltpu.VMEM((1, hid), f32),
            dma((8,)),
            pltpu.VMEM((HEADS // 2, UNIT * 4, 128), f32),
            pltpu.VMEM((HEADS, UNIT, 128), bf16),
            pltpu.VMEM((HEADS, UNIT // 2, 128), bf16),
            pltpu.VMEM((rows, dim), bf16),
            pltpu.VMEM((rows, 128), f32),
            pltpu.VMEM((4, 2, 512, 128), bf16),
            pltpu.VMEM((4, 2, 512, 128), bf16),
            pltpu.VMEM((4, 256, 128), bf16),
            pltpu.VMEM((4, 512, 256), bf16),
            pltpu.VMEM((4, 512, 128), f32),
            pltpu.VMEM((4, 8, 32, 128), bf16),
            pltpu.VMEM((8, 4, 32, 128), bf16),
            dma((2, 8)), dma((2, 8)), dma((3,)), dma((3,)), dma((3,)), dma((3,)),
            dma((4,)), dma((4,)), dma((4, 8)), dma((8, 4)),
        ],
        compiler_params=pltpu.CompilerParams(
            collective_id=0, has_side_effects=True, vmem_limit_bytes=56 << 20
        ),
        name="layer",
    )(
        projected, buckets.reshape(128, 128), time_table, out_weight, history,
        candidates.reshape(rows, dim), hidden_weight, score_weight.reshape(1, hid),
    )
    return layer, scores.T


def solution(mesh):
    rows = ("blk", "uly")
    return jax.shard_map(
        per_device,
        mesh=mesh,
        in_specs=(
            P(rows, None, None), P(rows, None), P(), P(), P(), P(rows, None, None), P(), P(),
        ),
        out_specs=(P(rows, None), P(rows, None)),
        check_vma=False,
    )
```

```python
import jax
import jax.numpy as jnp
from jax import lax
from jax.experimental import pallas as pl
from jax.experimental.pallas import tpu as pltpu
from jax.sharding import PartitionSpec as P

MESH = pl.DeviceIdType.MESH
NORM_EPS = 1e-05
DH = 64
CANDS = 8
UNIT = 64
HEADS = 8
HID_TILE = 1024
NB = 128
NT = (((1,), (1,)), ((), ()))


def device_at(x, y, z, core):
    return (x * 32 + y * 8 + lax.rem(z, 4) * 2 + core, z // 4)


def mirrored(row, col):
    return col + lax.rem(row, 2) * (3 - 2 * col)


def block_at(row, col):
    return 4 * mirrored(row, col) + row


def layer_kernel(
    projected_hbm, buckets_hbm, table_hbm, out_weight_hbm, history_hbm, candidates_hbm, hidden_hbm, score_hbm,
    layer_ref, scores_ref,
    projected, buckets_ref, table_ref, out_weight, history, candidates, hidden_weight, score_weight, load_sem,
    planes, kv_ref, q_ref, paired, score_acc,
    kv, keys_hot, q_packed, q_wide, acc, outgoing, returned,
    p1_send, p1_recv, kv_send, kv_recv, q_send, q_recv, twin_send, twin_recv, back_send, back_recv,
):
    blk, uly = lax.axis_index("blk"), lax.axis_index("uly")
    x, y = blk // 32, lax.rem(blk // 8, 4)
    z_lo, core = lax.rem(blk // 2, 4), lax.rem(blk, 2)
    z = uly * 4 + z_lo
    home_row, home_col = y, mirrored(y, x)
    target_x, target_y = home_col, home_row
    stays = y % 2 == 0
    row, col = y, x
    source_x, source_y = mirrored(row, col), row
    twin = device_at(x, y, z, 1 - core)

    early = mirrored(row, col) < 2
    key_steps = [
        jnp.int32(0), jnp.where(early, 2, 1), jnp.where(early, 1, 3), jnp.where(early, 3, 2),
    ]

    def along_col(d):
        return device_at(x, lax.rem(y + d, 4), z, core)

    def along_row(d):
        return device_at(lax.rem(x + d, 4), y, z, core)

    loads = [
        pltpu.make_async_copy(src, dst, load_sem.at[i])
        for i, (src, dst) in enumerate(
            (
                (projected_hbm, projected),
                (buckets_hbm, buckets_ref),
                (table_hbm, table_ref),
                (out_weight_hbm, out_weight),
                (history_hbm, history),
                (candidates_hbm, candidates),
                (score_hbm, score_weight),
                (hidden_hbm, hidden_weight),
            )
        )
    ]
    for load in loads[:3]:
        load.start()

    barrier = pltpu.get_barrier_semaphore()

    def greet(i, _):
        @pl.when(jnp.logical_not(jnp.logical_and(stays, i == z)))
        def _():
            pl.semaphore_signal(
                barrier, inc=1, device_id=device_at(source_x, source_y, i, core), device_id_type=MESH
            )

        return 0

    lax.fori_loop(0, 8, greet, 0)
    for d in range(1, 4):
        pl.semaphore_signal(barrier, inc=1, device_id=along_col(d), device_id_type=MESH)
        pl.semaphore_signal(barrier, inc=1, device_id=along_row(d), device_id_type=MESH)
    pl.semaphore_signal(barrier, inc=1, device_id=twin, device_id_type=MESH)

    low64 = lax.broadcasted_iota(jnp.int32, (UNIT, 128), 1) < DH
    low_half = lax.broadcasted_iota(jnp.int32, (UNIT // 2, 128), 1) < DH
    loads[0].wait()
    for group in range(HEADS // 2):
        lanes = slice(group * 128, group * 128 + 128)
        planes[group] = projected[:, :, lanes].astype(jnp.float32).reshape(UNIT * 4, 128)
        value, query, key = [planes[group, pl.ds(plane, UNIT, stride=4), :] for plane in (1, 2, 3)]
        kv_ref[2 * group] = jnp.where(low64, key, pltpu.roll(value, DH, 1)).astype(jnp.bfloat16)
        kv_ref[2 * group + 1] = jnp.where(low64, pltpu.roll(key, DH, 1), value).astype(jnp.bfloat16)
        early, late = query[:32] * 0.0625, query[32:] * 0.0625
        q_ref[2 * group] = jnp.where(low_half, early, pltpu.roll(late, DH, 1)).astype(jnp.bfloat16)
        q_ref[2 * group + 1] = jnp.where(low_half, pltpu.roll(early, DH, 1), late).astype(jnp.bfloat16)
    pl.semaphore_wait(barrier, 14 + lax.rem(y, 2))

    def unit_offset(zz):
        return lax.rem(zz, 4) * 2 + zz // 4

    def phase1_kv(head, src_z):
        return pltpu.make_async_remote_copy(
            src_ref=kv_ref.at[head],
            dst_ref=kv.at[home_row, core, pl.ds(pl.multiple_of(unit_offset(src_z) * 64, 64), 64)],
            send_sem=p1_send.at[0, head],
            recv_sem=p1_recv.at[src_z],
            device_id=device_at(target_x, target_y, head, core),
            device_id_type=MESH,
        )

    def phase1_q(head, src_z):
        return pltpu.make_async_remote_copy(
            src_ref=q_ref.at[head],
            dst_ref=q_packed.at[home_col, pl.ds(pl.multiple_of(unit_offset(src_z) * 32, 32), 32)],
            send_sem=p1_send.at[1, head],
            recv_sem=p1_recv.at[8 + src_z],
            device_id=device_at(target_x, target_y, head, core),
            device_id_type=MESH,
        )

    def arrived_kv(src_z):
        return pltpu.make_async_remote_copy(
            src_ref=kv_ref.at[0],
            dst_ref=kv.at[row, core, pl.ds(pl.multiple_of(unit_offset(src_z) * 64, 64), 64)],
            send_sem=p1_send.at[0, 0],
            recv_sem=p1_recv.at[src_z],
            device_id=device_at(source_x, source_y, src_z, core),
            device_id_type=MESH,
        )

    def arrived_q(src_z):
        return pltpu.make_async_remote_copy(
            src_ref=q_ref.at[0],
            dst_ref=q_packed.at[col, pl.ds(pl.multiple_of(unit_offset(src_z) * 32, 32), 32)],
            send_sem=p1_send.at[1, 0],
            recv_sem=p1_recv.at[8 + src_z],
            device_id=device_at(source_x, source_y, src_z, core),
            device_id_type=MESH,
        )

    def away(i):
        return lax.rem((i + 1) // 2 + lax.rem(i + 1, 2) * (8 - 2 * ((i + 1) // 2)) + 8, 8)

    def start_either(here, local, remote):
        @pl.when(here)
        def _():
            pltpu.make_async_copy(*local).start()

        @pl.when(jnp.logical_not(here))
        def _():
            remote().start()

    def send_first(i, _):
        head = lax.rem(z + away(i), 8)
        place = kv.at[home_row, core, pl.ds(pl.multiple_of(unit_offset(z) * 64, 64), 64)]
        start_either(
            jnp.logical_and(stays, head == z),
            (kv_ref.at[head], place, p1_recv.at[z]),
            lambda: phase1_kv(head, z),
        )
        place = q_packed.at[home_col, pl.ds(pl.multiple_of(unit_offset(z) * 32, 32), 32)]
        start_either(
            jnp.logical_and(stays, head == z),
            (q_ref.at[head], place, p1_recv.at[8 + z]),
            lambda: phase1_q(head, z),
        )
        return 0

    lax.fori_loop(0, 8, send_first, 0)
    for load in loads[3:]:
        load.start()
    for load in loads[1:3]:
        load.wait()

    lane = lax.broadcasted_iota(jnp.int32, (128, NB), 1)
    lane_f = lane.astype(jnp.float32)

    def bucket_columns(block):
        rows = buckets_ref[pl.ds(pl.multiple_of(block * 8, 8), 8), :]
        return jnp.transpose(rows.astype(jnp.float32))

    toeplitz = pltpu.roll(
        jnp.broadcast_to(table_ref[pl.ds(z, 1), :] * 0.5, (NB, NB)), 0, 1, stride=1, stride_axis=0
    ).astype(jnp.bfloat16)

    def key_columns(t, _):
        columns = bucket_columns(block_at(t, col))
        for stripe in range(8):
            hot = (columns[:, stripe : stripe + 1] == lane_f).astype(jnp.bfloat16)
            keys_hot[t, stripe % 2, (stripe // 2) * 128 : (stripe // 2 + 1) * 128, :] = hot
        return 0

    lax.fori_loop(0, 4, key_columns, 0)

    def query_columns(a, _):
        columns = bucket_columns(block_at(row, a))
        for stripe in range(4):
            own = jnp.where(
                core == 0, columns[:, 2 * stripe : 2 * stripe + 1], columns[:, 2 * stripe + 1 : 2 * stripe + 2]
            )
            hot = (own == lane_f).astype(jnp.bfloat16)
            bias = lax.dot_general(hot, toeplitz, NT, preferred_element_type=jnp.float32)
            bias = bias.astype(jnp.bfloat16).reshape(2, 2, 32, NB)
            for half in range(2):
                q_wide[a, half, stripe * 64 : stripe * 64 + 64, NB:] = bias[:, half].reshape(64, NB)
        acc[a] = jnp.zeros((2, 256, 128), jnp.float32)
        return 0

    lax.fori_loop(0, 4, query_columns, 0)

    def unpack_queries(a):
        packed = q_packed[a].astype(jnp.float32)
        low = lax.broadcasted_iota(jnp.int32, (256, 128), 1) < DH
        q_wide[a, 0, :, :NB] = jnp.where(low, packed, 0.0).astype(jnp.bfloat16)
        q_wide[a, 1, :, :NB] = jnp.where(low, pltpu.roll(packed, DH, 1), 0.0).astype(jnp.bfloat16)

    def kv_copy(slot, d):
        return pltpu.make_async_remote_copy(
            src_ref=kv.at[slot, core],
            dst_ref=kv.at[slot, core],
            send_sem=kv_send.at[d - 1],
            recv_sem=kv_recv.at[d - 1],
            device_id=along_col(d),
            device_id_type=MESH,
        )

    def q_copy(slot, d):
        return pltpu.make_async_remote_copy(
            src_ref=q_packed.at[slot],
            dst_ref=q_packed.at[slot],
            send_sem=q_send.at[d - 1],
            recv_sem=q_recv.at[d - 1],
            device_id=along_row(d),
            device_id_type=MESH,
        )

    def twin_copy(slot, half, d):
        return pltpu.make_async_remote_copy(
            src_ref=kv.at[slot, half],
            dst_ref=kv.at[slot, half],
            send_sem=twin_send.at[d],
            recv_sem=twin_recv.at[d],
            device_id=twin,
            device_id_type=MESH,
        )

    def forward(i, _):
        source = lax.rem(z + 8 - away(i), 8)
        arrived_kv(source).wait_recv()
        piece = kv.at[row, core, pl.ds(pl.multiple_of(unit_offset(source) * 64, 64), 64)]
        for d in key_steps[1:3]:
            pltpu.make_async_remote_copy(
                src_ref=piece, dst_ref=piece, send_sem=kv_send.at[d - 1], recv_sem=kv_recv.at[d - 1],
                device_id=along_col(d), device_id_type=MESH,
            ).start()
        arrived_q(source).wait_recv()
        packed = q_packed.at[col, pl.ds(pl.multiple_of(unit_offset(source) * 32, 32), 32)]
        for d in (1, 3, 2):
            pltpu.make_async_remote_copy(
                src_ref=packed, dst_ref=packed, send_sem=q_send.at[d - 1], recv_sem=q_recv.at[d - 1],
                device_id=along_row(d), device_id_type=MESH,
            ).start()
        pltpu.make_async_remote_copy(
            src_ref=piece, dst_ref=piece, send_sem=twin_send.at[0], recv_sem=twin_recv.at[0],
            device_id=twin, device_id_type=MESH,
        ).start()
        return 0

    lax.fori_loop(0, 8, forward, 0)
    kv_copy(row, key_steps[3]).start()
    unpack_queries(col)

    def activate(halved):
        return (halved + halved * jnp.tanh(halved)).astype(jnp.bfloat16)

    def attend_diagonal(key_core):
        held = kv[row, key_core]
        wide = jnp.concatenate([held, keys_hot[row, key_core]], axis=1)
        place_q = lax.broadcasted_iota(jnp.int32, (256, 512), 0)
        place_k = lax.broadcasted_iota(jnp.int32, (256, 512), 1)
        unit = place_q // 32
        event_q = (unit // 2) * 256 + (unit % 2) * 64 + core * 128 + place_q % 32
        event_k = place_k + (place_k // 128) * 128 + key_core * 128
        for half in range(2):
            scores = lax.dot_general(q_wide[col, half], wide, NT, preferred_element_type=jnp.float32)
            seen = event_k <= event_q + half * 32
            weights = jnp.where(seen, activate(scores), jnp.zeros((), jnp.bfloat16))
            acc[col, half] += jnp.dot(weights, held, preferred_element_type=jnp.float32)

    def attend(quarters, t, halves):
        held = kv[t].reshape(1024, 128)
        wide = jnp.concatenate([held, keys_hot[t].reshape(1024, 128)], axis=1)
        for quarter in quarters:
            a = mirrored(row, quarter)
            for half in halves:
                scores = lax.dot_general(q_wide[a, half], wide, NT, preferred_element_type=jnp.float32)
                acc[a, half] += jnp.dot(activate(scores), held, preferred_element_type=jnp.float32)

    def attend_all(t, halves, done=lambda quarter: None):
        first = mirrored(t, col) + jnp.where(row > t, 0, 1)
        odd = lax.rem(4 - first, 2)

        @pl.when(odd == 1)
        def _():
            attend([first], t, halves)
            done(first)

        def two(k, _):
            quarter = first + odd + 2 * k
            attend([quarter, quarter + 1], t, halves)
            done(quarter)
            done(quarter + 1)
            return 0

        lax.fori_loop(0, (4 - first) // 2, two, 0)
        return first

    def key_member(n):
        return lax.rem(row - key_steps[n] + 4, 4)

    attend_diagonal(core)
    twin_copy(row, 1 - core, 0).wait_recv()
    attend_diagonal(1 - core)

    def pass_on(d):
        t = lax.rem(row - d + 4, 4)
        kv_copy(t, d).wait_recv()
        twin_copy(t, core, d).start()

    def take_queries(d):
        a = lax.rem(col - d + 4, 4)
        q_copy(a, d).wait_recv()
        unpack_queries(a)

    def take_keys(d):
        twin_copy(lax.rem(row - d + 4, 4), 1 - core, d).wait_recv()

    pass_on(key_steps[1])
    pass_on(key_steps[2])
    for d in (1, 3, 2):
        take_queries(d)
    attend_all(row, (0, 1))
    take_keys(key_steps[1])
    attend_all(key_member(1), (0, 1))
    take_keys(key_steps[2])
    pass_on(key_steps[3])
    attend_all(key_member(2), (0, 1))
    take_keys(key_steps[3])

    low_units = lax.broadcasted_iota(jnp.int32, (8, 16, 128), 2) < DH

    def stays_back(a, unit):
        return jnp.logical_and(mirrored(row, a) == x, unit == unit_offset(z))

    def message(a, unit):
        return pl.ds(pl.multiple_of((a * 8 + unit) * 16, 16), 16)

    def send_quarter(half, quarter):
        a = mirrored(row, quarter)
        total = acc[a, half].reshape(8, 32, 128)
        total = jnp.where(low_units, pltpu.roll(total[:, :16], DH, 2), total[:, 16:]).astype(jnp.bfloat16)
        outgoing[half, pl.ds(pl.multiple_of(a * 128, 128), 128)] = total.reshape(128, 128)

        def send_back(unit, _):
            owner_z = lax.rem(unit, 2) * 4 + unit // 2
            source = outgoing.at[half, message(a, unit)]
            place = returned.at[half, z, col]
            start_either(
                stays_back(a, unit),
                (source, place, back_recv.at[half]),
                lambda: pltpu.make_async_remote_copy(
                    src_ref=source,
                    dst_ref=place,
                    send_sem=back_send.at[half],
                    recv_sem=back_recv.at[half],
                    device_id=device_at(mirrored(row, a), row, owner_z, core),
                    device_id_type=MESH,
                ),
            )
            return 0

        lax.fori_loop(0, 8, send_back, 0)

    def finish(half):
        def untouched(quarter, _):
            send_quarter(half, quarter)
            return 0

        t = key_member(3)
        lax.fori_loop(0, mirrored(t, col) + jnp.where(row > t, 0, 1), untouched, 0)
        attend_all(t, (half,), lambda quarter: send_quarter(half, quarter))

    finish(0)
    finish(1)

    def sent_first(i, _):
        @pl.when(jnp.logical_not(jnp.logical_and(stays, i == z)))
        def _():
            phase1_kv(i, z).wait_send()
            phase1_q(i, z).wait_send()

        return 0

    lax.fori_loop(0, 8, sent_first, 0)
    twin_copy(row, core, 0).wait_send()
    for d in range(1, 4):
        kv_copy(row, d).wait_send()
        q_copy(col, d).wait_send()
        twin_copy(lax.rem(row - d + 4, 4), core, d).wait_send()
    for load in loads[3:]:
        load.wait()

    low16 = lax.broadcasted_iota(jnp.int32, (16, 128), 1) < DH
    score_acc[...] = jnp.zeros_like(score_acc)

    def score_half(half):
        pltpu.make_async_copy(returned.at[half], returned.at[half], back_recv.at[half]).wait()
        sums = [
            jnp.sum(returned[half, h].astype(jnp.float32), axis=0).astype(jnp.bfloat16).astype(jnp.float32)
            for h in range(HEADS)
        ]
        parts = []
        for group in range(HEADS // 2):
            even, odd = sums[2 * group], sums[2 * group + 1]
            first = jnp.where(low16, even, pltpu.roll(odd, DH, 1))
            second = jnp.where(low16, pltpu.roll(even, DH, 1), odd)
            parts.append(jnp.concatenate([first, second], axis=0))
        restored = jnp.concatenate(parts, axis=1)
        centred = restored - jnp.mean(restored, axis=-1, keepdims=True)
        variance = jnp.mean(centred * centred, axis=-1, keepdims=True)
        normed = centred * lax.rsqrt(variance + NORM_EPS)
        gate = jnp.concatenate(
            [planes[group, pl.ds(half * 128, 32, stride=4), :] for group in range(HEADS // 2)], axis=1
        )
        gated = (normed * gate).astype(jnp.bfloat16)
        layer = jnp.dot(gated, out_weight[...], preferred_element_type=jnp.float32)
        layer = (layer + history[half * 32 : half * 32 + 32].astype(jnp.float32)).astype(jnp.bfloat16)
        layer_ref[half * 32 : half * 32 + 32] = layer
        halved_layer = layer.astype(jnp.float32) * 0.5
        for part in range(2):
            events = halved_layer[part * 16 : part * 16 + 16]
            rows = slice(half * 256 + part * 128, half * 256 + part * 128 + 128)
            spread = jnp.broadcast_to(events[:, None, :], (16, CANDS, events.shape[1])).reshape(128, -1)
            paired[rows] = (spread * candidates[rows].astype(jnp.float32)).astype(jnp.bfloat16)
        rows = slice(half * 256, half * 256 + 256)

        def score_tile(i, _):
            columns = pl.ds(pl.multiple_of(i * HID_TILE, HID_TILE), HID_TILE)
            halved = jnp.dot(paired[rows], hidden_weight[:, columns], preferred_element_type=jnp.float32)
            scored = (halved + halved * jnp.tanh(halved)) * score_weight[:, columns]
            total = score_acc[rows]
            for part in range(HID_TILE // 128):
                total += scored[:, part * 128 : part * 128 + 128]
            score_acc[rows] = total
            return 0

        lax.fori_loop(0, hidden_weight.shape[1] // HID_TILE, score_tile, 0)

    score_half(0)
    score_half(1)
    scores_ref[...] = jnp.transpose(jnp.sum(score_acc[...].reshape(UNIT, CANDS, 128), axis=-1))
    for half in range(2):
        left = outgoing.at[half, pl.ds(0, 31 * 16)]
        pltpu.make_async_copy(left, left, back_send.at[half]).wait()


def per_device(
    projected, history, buckets, time_table, out_weight, candidates, hidden_weight, score_weight
):
    width = projected.shape[2]
    dim = history.shape[1]
    hid = hidden_weight.shape[1]
    vmem = pl.BlockSpec(memory_space=pltpu.VMEM)
    hbm = pl.BlockSpec(memory_space=pl.ANY)
    dma = pltpu.SemaphoreType.DMA
    bf16, f32 = jnp.bfloat16, jnp.float32
    rows = UNIT * CANDS
    layer, scores = pl.pallas_call(
        layer_kernel,
        out_shape=(
            pltpu.VMEM((UNIT, dim), bf16),
            pltpu.VMEM((CANDS, UNIT), f32),
        ),
        in_specs=[hbm] * 8,
        out_specs=(vmem, vmem),
        scratch_shapes=[
            pltpu.VMEM((UNIT, 4, width), bf16),
            pltpu.VMEM((128, 128), jnp.int32),
            pltpu.VMEM((HEADS, NB), f32),
            pltpu.VMEM((width, dim), bf16),
            pltpu.VMEM((UNIT, dim), bf16),
            pltpu.VMEM((rows, dim), bf16),
            pltpu.VMEM((dim, hid), bf16),
            pltpu.VMEM((1, hid), f32),
            dma((8,)),
            pltpu.VMEM((HEADS // 2, UNIT * 4, 128), f32),
            pltpu.VMEM((HEADS, UNIT, 128), bf16),
            pltpu.VMEM((HEADS, UNIT // 2, 128), bf16),
            pltpu.VMEM((rows, dim), bf16),
            pltpu.VMEM((rows, 128), f32),
            pltpu.VMEM((4, 2, 512, 128), bf16),
            pltpu.VMEM((4, 2, 512, 128), bf16),
            pltpu.VMEM((4, 256, 128), bf16),
            pltpu.VMEM((4, 2, 256, 256), bf16),
            pltpu.VMEM((4, 2, 256, 128), f32),
            pltpu.VMEM((2, 512, 128), bf16),
            pltpu.VMEM((2, 8, 4, 16, 128), bf16),
            dma((2, 8)), dma((16,)), dma((3,)), dma((3,)), dma((3,)), dma((3,)),
            dma((4,)), dma((4,)), dma((2,)), dma((2,)),
        ],
        compiler_params=pltpu.CompilerParams(
            collective_id=0, has_side_effects=True, vmem_limit_bytes=56 << 20
        ),
        name="layer",
    )(
        projected, buckets.reshape(128, 128), time_table, out_weight, history,
        candidates.reshape(rows, dim), hidden_weight, score_weight.reshape(1, hid),
    )
    return layer, scores.T


def solution(mesh):
    rows = ("blk", "uly")
    return jax.shard_map(
        per_device,
        mesh=mesh,
        in_specs=(
            P(rows, None, None), P(rows, None), P(), P(), P(), P(rows, None, None), P(), P(),
        ),
        out_specs=(P(rows, None), P(rows, None)),
        check_vma=False,
    )
```

```python
import jax
import jax.numpy as jnp
from jax import lax
from jax.experimental import pallas as pl
from jax.experimental.pallas import tpu as pltpu
from jax.sharding import PartitionSpec as P

MESH = pl.DeviceIdType.MESH
NORM_EPS = 1e-05
DH = 64
CANDS = 8
UNIT = 64
HEADS = 8
HID_TILE = 2048
NB = 128
NT = (((1,), (1,)), ((), ()))


def device_at(x, y, z, core):
    return (x * 32 + y * 8 + lax.rem(z, 4) * 2 + core, z // 4)


def mirrored(row, col):
    return col + lax.rem(row, 2) * (3 - 2 * col)


def block_at(row, col):
    return 4 * mirrored(row, col) + row


def layer_kernel(
    projected_hbm, buckets_hbm, table_hbm, out_weight_hbm, history_hbm, candidates_hbm, hidden_hbm, score_hbm,
    layer_ref, scores_ref,
    projected, buckets_ref, table_ref, out_weight, history, candidates, hidden_weight, score_weight, load_sem,
    planes, kv_ref, q_ref, paired, score_acc,
    kv, keys_hot, q_packed, q_wide, acc, outgoing, returned,
    p1_send, p1_recv, kv_send, kv_recv, q_send, q_recv, twin_send, twin_recv, back_send, back_recv,
):
    blk, uly = lax.axis_index("blk"), lax.axis_index("uly")
    x, y = blk // 32, lax.rem(blk // 8, 4)
    z_lo, core = lax.rem(blk // 2, 4), lax.rem(blk, 2)
    z = uly * 4 + z_lo
    home_row, home_col = y, mirrored(y, x)
    target_x, target_y = home_col, home_row
    stays = y % 2 == 0
    row, col = y, x
    source_x, source_y = mirrored(row, col), row
    twin = device_at(x, y, z, 1 - core)

    early = mirrored(row, col) < 2
    key_steps = [
        jnp.int32(0), jnp.where(early, 2, 1), jnp.where(early, 1, 3), jnp.where(early, 3, 2),
    ]

    def along_col(d):
        return device_at(x, lax.rem(y + d, 4), z, core)

    def along_row(d):
        return device_at(lax.rem(x + d, 4), y, z, core)

    loads = [
        pltpu.make_async_copy(src, dst, load_sem.at[i])
        for i, (src, dst) in enumerate(
            (
                (projected_hbm, projected),
                (buckets_hbm, buckets_ref),
                (table_hbm, table_ref),
                (out_weight_hbm, out_weight),
                (history_hbm, history),
                (candidates_hbm, candidates),
                (score_hbm, score_weight),
                (hidden_hbm, hidden_weight),
            )
        )
    ]
    for load in loads[:3]:
        load.start()

    barrier = pltpu.get_barrier_semaphore()

    def greet(i, _):
        @pl.when(jnp.logical_not(jnp.logical_and(stays, i == z)))
        def _():
            pl.semaphore_signal(
                barrier, inc=1, device_id=device_at(source_x, source_y, i, core), device_id_type=MESH
            )

        return 0

    lax.fori_loop(0, 8, greet, 0)
    for d in range(1, 4):
        pl.semaphore_signal(barrier, inc=1, device_id=along_col(d), device_id_type=MESH)
        pl.semaphore_signal(barrier, inc=1, device_id=along_row(d), device_id_type=MESH)
    pl.semaphore_signal(barrier, inc=1, device_id=twin, device_id_type=MESH)

    low64 = lax.broadcasted_iota(jnp.int32, (UNIT, 128), 1) < DH
    low_half = lax.broadcasted_iota(jnp.int32, (UNIT // 2, 128), 1) < DH
    loads[0].wait()
    for group in range(HEADS // 2):
        lanes = slice(group * 128, group * 128 + 128)
        planes[group] = projected[:, :, lanes].astype(jnp.float32).reshape(UNIT * 4, 128)
        value, query, key = [planes[group, pl.ds(plane, UNIT, stride=4), :] for plane in (1, 2, 3)]
        kv_ref[2 * group] = jnp.where(low64, key, pltpu.roll(value, DH, 1)).astype(jnp.bfloat16)
        kv_ref[2 * group + 1] = jnp.where(low64, pltpu.roll(key, DH, 1), value).astype(jnp.bfloat16)
        early, late = query[:32] * 0.0625, query[32:] * 0.0625
        q_ref[2 * group] = jnp.where(low_half, early, pltpu.roll(late, DH, 1)).astype(jnp.bfloat16)
        q_ref[2 * group + 1] = jnp.where(low_half, pltpu.roll(early, DH, 1), late).astype(jnp.bfloat16)
    pl.semaphore_wait(barrier, 14 + lax.rem(y, 2))

    def unit_offset(zz):
        return lax.rem(zz, 4) * 2 + zz // 4

    def phase1_kv(head, src_z):
        return pltpu.make_async_remote_copy(
            src_ref=kv_ref.at[head],
            dst_ref=kv.at[home_row, core, pl.ds(pl.multiple_of(unit_offset(src_z) * 64, 64), 64)],
            send_sem=p1_send.at[0, head],
            recv_sem=p1_recv.at[src_z],
            device_id=device_at(target_x, target_y, head, core),
            device_id_type=MESH,
        )

    def phase1_q(head, src_z):
        return pltpu.make_async_remote_copy(
            src_ref=q_ref.at[head],
            dst_ref=q_packed.at[home_col, pl.ds(pl.multiple_of(unit_offset(src_z) * 32, 32), 32)],
            send_sem=p1_send.at[1, head],
            recv_sem=p1_recv.at[8 + src_z],
            device_id=device_at(target_x, target_y, head, core),
            device_id_type=MESH,
        )

    def arrived_kv(src_z):
        return pltpu.make_async_remote_copy(
            src_ref=kv_ref.at[0],
            dst_ref=kv.at[row, core, pl.ds(pl.multiple_of(unit_offset(src_z) * 64, 64), 64)],
            send_sem=p1_send.at[0, 0],
            recv_sem=p1_recv.at[src_z],
            device_id=device_at(source_x, source_y, src_z, core),
            device_id_type=MESH,
        )

    def arrived_q(src_z):
        return pltpu.make_async_remote_copy(
            src_ref=q_ref.at[0],
            dst_ref=q_packed.at[col, pl.ds(pl.multiple_of(unit_offset(src_z) * 32, 32), 32)],
            send_sem=p1_send.at[1, 0],
            recv_sem=p1_recv.at[8 + src_z],
            device_id=device_at(source_x, source_y, src_z, core),
            device_id_type=MESH,
        )

    def away(i):
        return lax.rem((i + 1) // 2 + lax.rem(i + 1, 2) * (8 - 2 * ((i + 1) // 2)) + 8, 8)

    def start_either(here, local, remote):
        @pl.when(here)
        def _():
            pltpu.make_async_copy(*local).start()

        @pl.when(jnp.logical_not(here))
        def _():
            remote().start()

    def send_first(i, _):
        head = lax.rem(z + away(i), 8)
        place = kv.at[home_row, core, pl.ds(pl.multiple_of(unit_offset(z) * 64, 64), 64)]
        start_either(
            jnp.logical_and(stays, head == z),
            (kv_ref.at[head], place, p1_recv.at[z]),
            lambda: phase1_kv(head, z),
        )
        place = q_packed.at[home_col, pl.ds(pl.multiple_of(unit_offset(z) * 32, 32), 32)]
        start_either(
            jnp.logical_and(stays, head == z),
            (q_ref.at[head], place, p1_recv.at[8 + z]),
            lambda: phase1_q(head, z),
        )
        return 0

    lax.fori_loop(0, 8, send_first, 0)
    for load in loads[3:]:
        load.start()
    for load in loads[1:3]:
        load.wait()

    lane = lax.broadcasted_iota(jnp.int32, (128, NB), 1)
    lane_f = lane.astype(jnp.float32)

    def bucket_columns(block):
        rows = buckets_ref[pl.ds(pl.multiple_of(block * 8, 8), 8), :]
        return jnp.transpose(rows.astype(jnp.float32))

    toeplitz = pltpu.roll(
        jnp.broadcast_to(table_ref[pl.ds(z, 1), :] * 0.5, (NB, NB)), 0, 1, stride=1, stride_axis=0
    ).astype(jnp.bfloat16)

    def key_columns(t, _):
        columns = bucket_columns(block_at(t, col))
        for stripe in range(8):
            hot = (columns[:, stripe : stripe + 1] == lane_f).astype(jnp.bfloat16)
            keys_hot[t, stripe % 2, (stripe // 2) * 128 : (stripe // 2 + 1) * 128, :] = hot
        return 0

    lax.fori_loop(0, 4, key_columns, 0)

    def query_columns(a, _):
        columns = bucket_columns(block_at(row, a))
        for stripe in range(4):
            own = jnp.where(
                core == 0, columns[:, 2 * stripe : 2 * stripe + 1], columns[:, 2 * stripe + 1 : 2 * stripe + 2]
            )
            hot = (own == lane_f).astype(jnp.bfloat16)
            bias = lax.dot_general(hot, toeplitz, NT, preferred_element_type=jnp.float32)
            bias = bias.astype(jnp.bfloat16).reshape(2, 2, 32, NB)
            for half in range(2):
                q_wide[a, half, stripe * 64 : stripe * 64 + 64, NB:] = bias[:, half].reshape(64, NB)
        acc[a] = jnp.zeros((2, 256, 128), jnp.float32)
        return 0

    lax.fori_loop(0, 4, query_columns, 0)

    def unpack_queries(a):
        packed = q_packed[a].astype(jnp.float32)
        low = lax.broadcasted_iota(jnp.int32, (256, 128), 1) < DH
        q_wide[a, 0, :, :NB] = jnp.where(low, packed, 0.0).astype(jnp.bfloat16)
        q_wide[a, 1, :, :NB] = jnp.where(low, pltpu.roll(packed, DH, 1), 0.0).astype(jnp.bfloat16)

    def kv_copy(slot, d):
        return pltpu.make_async_remote_copy(
            src_ref=kv.at[slot, core],
            dst_ref=kv.at[slot, core],
            send_sem=kv_send.at[d - 1],
            recv_sem=kv_recv.at[d - 1],
            device_id=along_col(d),
            device_id_type=MESH,
        )

    def q_copy(slot, d):
        return pltpu.make_async_remote_copy(
            src_ref=q_packed.at[slot],
            dst_ref=q_packed.at[slot],
            send_sem=q_send.at[d - 1],
            recv_sem=q_recv.at[d - 1],
            device_id=along_row(d),
            device_id_type=MESH,
        )

    def twin_copy(slot, half, d):
        return pltpu.make_async_remote_copy(
            src_ref=kv.at[slot, half],
            dst_ref=kv.at[slot, half],
            send_sem=twin_send.at[d],
            recv_sem=twin_recv.at[d],
            device_id=twin,
            device_id_type=MESH,
        )

    def forward(i, _):
        source = lax.rem(z + 8 - away(i), 8)
        arrived_kv(source).wait_recv()
        piece = kv.at[row, core, pl.ds(pl.multiple_of(unit_offset(source) * 64, 64), 64)]
        for d in key_steps[1:3]:
            pltpu.make_async_remote_copy(
                src_ref=piece, dst_ref=piece, send_sem=kv_send.at[d - 1], recv_sem=kv_recv.at[d - 1],
                device_id=along_col(d), device_id_type=MESH,
            ).start()
        arrived_q(source).wait_recv()
        packed = q_packed.at[col, pl.ds(pl.multiple_of(unit_offset(source) * 32, 32), 32)]
        for d in (1, 3, 2):
            pltpu.make_async_remote_copy(
                src_ref=packed, dst_ref=packed, send_sem=q_send.at[d - 1], recv_sem=q_recv.at[d - 1],
                device_id=along_row(d), device_id_type=MESH,
            ).start()
        pltpu.make_async_remote_copy(
            src_ref=piece, dst_ref=piece, send_sem=twin_send.at[0], recv_sem=twin_recv.at[0],
            device_id=twin, device_id_type=MESH,
        ).start()
        return 0

    lax.fori_loop(0, 8, forward, 0)
    kv_copy(row, key_steps[3]).start()
    unpack_queries(col)

    def activate(halved):
        return (halved + halved * jnp.tanh(halved)).astype(jnp.bfloat16)

    def attend_diagonal(unit0, keys):
        rows = slice(unit0 * 32, unit0 * 32 + 128)
        held = jnp.concatenate([kv[row, 0, :keys], kv[row, 1, :keys]], axis=0)
        hot = jnp.concatenate([keys_hot[row, 0, :keys], keys_hot[row, 1, :keys]], axis=0)
        wide = jnp.concatenate([held, hot], axis=1)
        query = jnp.concatenate([q_wide[col, 0, rows], q_wide[col, 1, rows]], axis=0)
        scores = lax.dot_general(query, wide, NT, preferred_element_type=jnp.float32)
        place_q = lax.broadcasted_iota(jnp.int32, (256, 1), 0)
        unit = unit0 + (place_q % 128) // 32
        event_q = (unit // 2) * 256 + (unit % 2) * 64 + core * 128 + (place_q // 128) * 32 + place_q % 32
        place_k = lax.broadcasted_iota(jnp.int32, (1, 2 * keys), 1)
        event_k = ((place_k % keys) // 128) * 256 + (place_k // keys) * 128 + place_k % 128
        weights = jnp.where(event_k <= event_q, activate(scores), jnp.zeros((), jnp.bfloat16))
        total = jnp.dot(weights, held, preferred_element_type=jnp.float32)
        acc[col, 0, rows] += total[:128]
        acc[col, 1, rows] += total[128:]

    def attend(quarters, t, halves):
        held = kv[t].reshape(1024, 128)
        wide = jnp.concatenate([held, keys_hot[t].reshape(1024, 128)], axis=1)
        for quarter in quarters:
            a = mirrored(row, quarter)
            for half in halves:
                scores = lax.dot_general(q_wide[a, half], wide, NT, preferred_element_type=jnp.float32)
                acc[a, half] += jnp.dot(activate(scores), held, preferred_element_type=jnp.float32)

    def attend_all(t, halves, done=lambda quarter: None):
        first = mirrored(t, col) + jnp.where(row > t, 0, 1)
        odd = lax.rem(4 - first, 2)

        @pl.when(odd == 1)
        def _():
            attend([first], t, halves)
            done(first)

        def two(k, _):
            quarter = first + odd + 2 * k
            attend([quarter, quarter + 1], t, halves)
            done(quarter)
            done(quarter + 1)
            return 0

        lax.fori_loop(0, (4 - first) // 2, two, 0)
        return first

    def key_member(n):
        return lax.rem(row - key_steps[n] + 4, 4)

    twin_copy(row, 1 - core, 0).wait_recv()
    attend_diagonal(0, 256)
    attend_diagonal(4, 512)

    def pass_on(d):
        t = lax.rem(row - d + 4, 4)
        kv_copy(t, d).wait_recv()
        twin_copy(t, core, d).start()

    def take_queries(d):
        a = lax.rem(col - d + 4, 4)
        q_copy(a, d).wait_recv()
        unpack_queries(a)

    def take_keys(d):
        twin_copy(lax.rem(row - d + 4, 4), 1 - core, d).wait_recv()

    pass_on(key_steps[1])
    pass_on(key_steps[2])
    for d in (1, 3, 2):
        take_queries(d)
    attend_all(row, (0, 1))
    take_keys(key_steps[1])
    attend_all(key_member(1), (0, 1))
    take_keys(key_steps[2])
    pass_on(key_steps[3])
    attend_all(key_member(2), (0, 1))
    take_keys(key_steps[3])

    low_units = lax.broadcasted_iota(jnp.int32, (8, 16, 128), 2) < DH

    def stays_back(a, unit):
        return jnp.logical_and(mirrored(row, a) == x, unit == unit_offset(z))

    def message(a, unit):
        return pl.ds(pl.multiple_of((a * 8 + unit) * 16, 16), 16)

    def send_quarter(half, quarter):
        a = mirrored(row, quarter)
        total = acc[a, half].reshape(8, 32, 128)
        total = jnp.where(low_units, pltpu.roll(total[:, :16], DH, 2), total[:, 16:]).astype(jnp.bfloat16)
        outgoing[half, pl.ds(pl.multiple_of(a * 128, 128), 128)] = total.reshape(128, 128)

        def send_back(i, _):
            owner_z = lax.rem(z + away(7 - i), 8)
            unit = unit_offset(owner_z)
            source = outgoing.at[half, message(a, unit)]
            place = returned.at[half, z, col]
            start_either(
                stays_back(a, unit),
                (source, place, back_recv.at[half]),
                lambda: pltpu.make_async_remote_copy(
                    src_ref=source,
                    dst_ref=place,
                    send_sem=back_send.at[half],
                    recv_sem=back_recv.at[half],
                    device_id=device_at(mirrored(row, a), row, owner_z, core),
                    device_id_type=MESH,
                ),
            )
            return 0

        lax.fori_loop(0, 8, send_back, 0)

    def finish(half):
        def untouched(quarter, _):
            send_quarter(half, quarter)
            return 0

        t = key_member(3)
        lax.fori_loop(0, mirrored(t, col) + jnp.where(row > t, 0, 1), untouched, 0)
        attend_all(t, (half,), lambda quarter: send_quarter(half, quarter))

    finish(0)
    finish(1)

    def sent_first(i, _):
        @pl.when(jnp.logical_not(jnp.logical_and(stays, i == z)))
        def _():
            phase1_kv(i, z).wait_send()
            phase1_q(i, z).wait_send()

        return 0

    lax.fori_loop(0, 8, sent_first, 0)
    twin_copy(row, core, 0).wait_send()
    for d in range(1, 4):
        kv_copy(row, d).wait_send()
        q_copy(col, d).wait_send()
        twin_copy(lax.rem(row - d + 4, 4), core, d).wait_send()
    for load in loads[3:]:
        load.wait()

    low16 = lax.broadcasted_iota(jnp.int32, (16, 128), 1) < DH
    score_acc[...] = jnp.zeros_like(score_acc)

    def score_half(half):
        pltpu.make_async_copy(returned.at[half], returned.at[half], back_recv.at[half]).wait()
        sums = [
            jnp.sum(returned[half, h].astype(jnp.float32), axis=0).astype(jnp.bfloat16).astype(jnp.float32)
            for h in range(HEADS)
        ]
        parts = []
        for group in range(HEADS // 2):
            even, odd = sums[2 * group], sums[2 * group + 1]
            first = jnp.where(low16, even, pltpu.roll(odd, DH, 1))
            second = jnp.where(low16, pltpu.roll(even, DH, 1), odd)
            parts.append(jnp.concatenate([first, second], axis=0))
        restored = jnp.concatenate(parts, axis=1)
        centred = restored - jnp.mean(restored, axis=-1, keepdims=True)
        variance = jnp.mean(centred * centred, axis=-1, keepdims=True)
        normed = centred * lax.rsqrt(variance + NORM_EPS)
        gate = jnp.concatenate(
            [planes[group, pl.ds(half * 128, 32, stride=4), :] for group in range(HEADS // 2)], axis=1
        )
        gated = (normed * gate).astype(jnp.bfloat16)
        layer = jnp.dot(gated, out_weight[...], preferred_element_type=jnp.float32)
        layer = (layer + history[half * 32 : half * 32 + 32].astype(jnp.float32)).astype(jnp.bfloat16)
        layer_ref[half * 32 : half * 32 + 32] = layer
        halved_layer = layer.astype(jnp.float32) * 0.5
        for part in range(2):
            events = halved_layer[part * 16 : part * 16 + 16]
            rows = slice(half * 256 + part * 128, half * 256 + part * 128 + 128)
            spread = jnp.broadcast_to(events[:, None, :], (16, CANDS, events.shape[1])).reshape(128, -1)
            paired[rows] = (spread * candidates[rows].astype(jnp.float32)).astype(jnp.bfloat16)
        rows = slice(half * 256, half * 256 + 256)

        def score_tile(i, _):
            columns = pl.ds(pl.multiple_of(i * HID_TILE, HID_TILE), HID_TILE)
            halved = jnp.dot(paired[rows], hidden_weight[:, columns], preferred_element_type=jnp.float32)
            scored = (halved + halved * jnp.tanh(halved)) * score_weight[:, columns]
            total = score_acc[rows]
            for part in range(HID_TILE // 128):
                total += scored[:, part * 128 : part * 128 + 128]
            score_acc[rows] = total
            return 0

        lax.fori_loop(0, hidden_weight.shape[1] // HID_TILE, score_tile, 0)

    score_half(0)
    score_half(1)
    scores_ref[...] = jnp.transpose(jnp.sum(score_acc[...].reshape(UNIT, CANDS, 128), axis=-1))
    for half in range(2):
        left = outgoing.at[half, pl.ds(0, 31 * 16)]
        pltpu.make_async_copy(left, left, back_send.at[half]).wait()


def per_device(
    projected, history, buckets, time_table, out_weight, candidates, hidden_weight, score_weight
):
    width = projected.shape[2]
    dim = history.shape[1]
    hid = hidden_weight.shape[1]
    vmem = pl.BlockSpec(memory_space=pltpu.VMEM)
    hbm = pl.BlockSpec(memory_space=pl.ANY)
    dma = pltpu.SemaphoreType.DMA
    bf16, f32 = jnp.bfloat16, jnp.float32
    rows = UNIT * CANDS
    layer, scores = pl.pallas_call(
        layer_kernel,
        out_shape=(
            pltpu.VMEM((UNIT, dim), bf16),
            pltpu.VMEM((CANDS, UNIT), f32),
        ),
        in_specs=[hbm] * 8,
        out_specs=(vmem, vmem),
        scratch_shapes=[
            pltpu.VMEM((UNIT, 4, width), bf16),
            pltpu.VMEM((128, 128), jnp.int32),
            pltpu.VMEM((HEADS, NB), f32),
            pltpu.VMEM((width, dim), bf16),
            pltpu.VMEM((UNIT, dim), bf16),
            pltpu.VMEM((rows, dim), bf16),
            pltpu.VMEM((dim, hid), bf16),
            pltpu.VMEM((1, hid), f32),
            dma((8,)),
            pltpu.VMEM((HEADS // 2, UNIT * 4, 128), f32),
            pltpu.VMEM((HEADS, UNIT, 128), bf16),
            pltpu.VMEM((HEADS, UNIT // 2, 128), bf16),
            pltpu.VMEM((rows, dim), bf16),
            pltpu.VMEM((rows, 128), f32),
            pltpu.VMEM((4, 2, 512, 128), bf16),
            pltpu.VMEM((4, 2, 512, 128), bf16),
            pltpu.VMEM((4, 256, 128), bf16),
            pltpu.VMEM((4, 2, 256, 256), bf16),
            pltpu.VMEM((4, 2, 256, 128), f32),
            pltpu.VMEM((2, 512, 128), bf16),
            pltpu.VMEM((2, 8, 4, 16, 128), bf16),
            dma((2, 8)), dma((16,)), dma((3,)), dma((3,)), dma((3,)), dma((3,)),
            dma((4,)), dma((4,)), dma((2,)), dma((2,)),
        ],
        compiler_params=pltpu.CompilerParams(
            collective_id=0, has_side_effects=True, vmem_limit_bytes=56 << 20
        ),
        name="layer",
    )(
        projected, buckets.reshape(128, 128), time_table, out_weight, history,
        candidates.reshape(rows, dim), hidden_weight, score_weight.reshape(1, hid),
    )
    return layer, scores.T


def solution(mesh):
    rows = ("blk", "uly")
    return jax.shard_map(
        per_device,
        mesh=mesh,
        in_specs=(
            P(rows, None, None), P(rows, None), P(), P(), P(), P(rows, None, None), P(), P(),
        ),
        out_specs=(P(rows, None), P(rows, None)),
        check_vma=False,
    )
```

```python
import jax
import jax.numpy as jnp
from jax import lax
from jax.experimental import pallas as pl
from jax.experimental.pallas import tpu as pltpu
from jax.sharding import PartitionSpec as P

MESH = pl.DeviceIdType.MESH
NORM_EPS = 1e-05
DH = 64
CANDS = 8
UNIT = 64
HEADS = 8
HID_TILE = 2048
NB = 128
NT = (((1,), (1,)), ((), ()))


def device_at(x, y, z, core):
    return (x * 32 + y * 8 + lax.rem(z, 4) * 2 + core, z // 4)


def mirrored(row, col):
    return col + lax.rem(row, 2) * (3 - 2 * col)


def block_at(row, col):
    return 4 * mirrored(row, col) + row


def layer_kernel(
    projected_hbm, buckets_hbm, table_hbm, out_weight_hbm, history_hbm, candidates_hbm, hidden_hbm, score_hbm,
    layer_ref, scores_ref,
    projected, buckets_ref, table_ref, out_weight, history, candidates, hidden_weight, score_weight, load_sem,
    planes, kv_ref, q_ref, paired, score_acc,
    kv, keys_hot, q_packed, q_wide, acc, outgoing, returned,
    p1_send, p1_recv, kv_send, kv_recv, q_send, q_recv, twin_send, twin_recv, back_send, back_recv,
):
    blk, uly = lax.axis_index("blk"), lax.axis_index("uly")
    x, y = blk // 32, lax.rem(blk // 8, 4)
    z_lo, core = lax.rem(blk // 2, 4), lax.rem(blk, 2)
    z = uly * 4 + z_lo
    home_row, home_col = y, mirrored(y, x)
    target_x, target_y = home_col, home_row
    stays = y % 2 == 0
    row, col = y, x
    source_x, source_y = mirrored(row, col), row
    twin = device_at(x, y, z, 1 - core)

    early = mirrored(row, col) < 2
    key_steps = [
        jnp.int32(0), jnp.where(early, 2, 1), jnp.where(early, 1, 3), jnp.where(early, 3, 2),
    ]

    def along_col(d):
        return device_at(x, lax.rem(y + d, 4), z, core)

    def along_row(d):
        return device_at(lax.rem(x + d, 4), y, z, core)

    loads = [
        pltpu.make_async_copy(src, dst, load_sem.at[i])
        for i, (src, dst) in enumerate(
            (
                (projected_hbm, projected),
                (buckets_hbm, buckets_ref),
                (table_hbm, table_ref),
                (out_weight_hbm, out_weight),
                (history_hbm, history),
                (candidates_hbm, candidates),
                (score_hbm, score_weight),
                (hidden_hbm, hidden_weight),
            )
        )
    ]
    for load in loads[:3]:
        load.start()

    barrier = pltpu.get_barrier_semaphore()

    def greet(i, _):
        @pl.when(jnp.logical_not(jnp.logical_and(stays, i == z)))
        def _():
            pl.semaphore_signal(
                barrier, inc=1, device_id=device_at(source_x, source_y, i, core), device_id_type=MESH
            )

        return 0

    lax.fori_loop(0, 8, greet, 0, unroll=True)
    for d in range(1, 4):
        pl.semaphore_signal(barrier, inc=1, device_id=along_col(d), device_id_type=MESH)
        pl.semaphore_signal(barrier, inc=1, device_id=along_row(d), device_id_type=MESH)
    pl.semaphore_signal(barrier, inc=1, device_id=twin, device_id_type=MESH)

    low64 = lax.broadcasted_iota(jnp.int32, (UNIT, 128), 1) < DH
    low_half = lax.broadcasted_iota(jnp.int32, (UNIT // 2, 128), 1) < DH
    loads[0].wait()
    for group in range(HEADS // 2):
        lanes = slice(group * 128, group * 128 + 128)
        planes[group] = projected[:, :, lanes].astype(jnp.float32).reshape(UNIT * 4, 128)
        value, query, key = [planes[group, pl.ds(plane, UNIT, stride=4), :] for plane in (1, 2, 3)]
        kv_ref[2 * group] = jnp.where(low64, key, pltpu.roll(value, DH, 1)).astype(jnp.bfloat16)
        kv_ref[2 * group + 1] = jnp.where(low64, pltpu.roll(key, DH, 1), value).astype(jnp.bfloat16)
        early, late = query[:32] * 0.0625, query[32:] * 0.0625
        q_ref[2 * group] = jnp.where(low_half, early, pltpu.roll(late, DH, 1)).astype(jnp.bfloat16)
        q_ref[2 * group + 1] = jnp.where(low_half, pltpu.roll(early, DH, 1), late).astype(jnp.bfloat16)
    pl.semaphore_wait(barrier, 14 + lax.rem(y, 2))

    def unit_offset(zz):
        return lax.rem(zz, 4) * 2 + zz // 4

    def phase1_kv(head, src_z):
        return pltpu.make_async_remote_copy(
            src_ref=kv_ref.at[head],
            dst_ref=kv.at[home_row, core, pl.ds(pl.multiple_of(unit_offset(src_z) * 64, 64), 64)],
            send_sem=p1_send.at[0, head],
            recv_sem=p1_recv.at[src_z],
            device_id=device_at(target_x, target_y, head, core),
            device_id_type=MESH,
        )

    def phase1_q(head, src_z):
        return pltpu.make_async_remote_copy(
            src_ref=q_ref.at[head],
            dst_ref=q_packed.at[home_col, pl.ds(pl.multiple_of(unit_offset(src_z) * 32, 32), 32)],
            send_sem=p1_send.at[1, head],
            recv_sem=p1_recv.at[8 + src_z],
            device_id=device_at(target_x, target_y, head, core),
            device_id_type=MESH,
        )

    def arrived_kv(src_z):
        return pltpu.make_async_remote_copy(
            src_ref=kv_ref.at[0],
            dst_ref=kv.at[row, core, pl.ds(pl.multiple_of(unit_offset(src_z) * 64, 64), 64)],
            send_sem=p1_send.at[0, 0],
            recv_sem=p1_recv.at[src_z],
            device_id=device_at(source_x, source_y, src_z, core),
            device_id_type=MESH,
        )

    def arrived_q(src_z):
        return pltpu.make_async_remote_copy(
            src_ref=q_ref.at[0],
            dst_ref=q_packed.at[col, pl.ds(pl.multiple_of(unit_offset(src_z) * 32, 32), 32)],
            send_sem=p1_send.at[1, 0],
            recv_sem=p1_recv.at[8 + src_z],
            device_id=device_at(source_x, source_y, src_z, core),
            device_id_type=MESH,
        )

    def away(i):
        return lax.rem((i + 1) // 2 + lax.rem(i + 1, 2) * (8 - 2 * ((i + 1) // 2)) + 8, 8)

    def start_either(here, local, remote):
        @pl.when(here)
        def _():
            pltpu.make_async_copy(*local).start()

        @pl.when(jnp.logical_not(here))
        def _():
            remote().start()

    def send_first(i, _):
        head = lax.rem(z + away(i), 8)
        place = kv.at[home_row, core, pl.ds(pl.multiple_of(unit_offset(z) * 64, 64), 64)]
        start_either(
            jnp.logical_and(stays, head == z),
            (kv_ref.at[head], place, p1_recv.at[z]),
            lambda: phase1_kv(head, z),
        )
        place = q_packed.at[home_col, pl.ds(pl.multiple_of(unit_offset(z) * 32, 32), 32)]
        start_either(
            jnp.logical_and(stays, head == z),
            (q_ref.at[head], place, p1_recv.at[8 + z]),
            lambda: phase1_q(head, z),
        )
        return 0

    lax.fori_loop(0, 8, send_first, 0, unroll=True)
    for load in loads[3:]:
        load.start()
    for load in loads[1:3]:
        load.wait()

    lane = lax.broadcasted_iota(jnp.int32, (128, NB), 1)
    lane_f = lane.astype(jnp.float32)

    def bucket_columns(block):
        rows = buckets_ref[pl.ds(pl.multiple_of(block * 8, 8), 8), :]
        return jnp.transpose(rows.astype(jnp.float32))

    toeplitz = pltpu.roll(
        jnp.broadcast_to(table_ref[pl.ds(z, 1), :] * 0.5, (NB, NB)), 0, 1, stride=1, stride_axis=0
    ).astype(jnp.bfloat16)

    def key_columns(t, _):
        columns = bucket_columns(block_at(t, col))
        for stripe in range(8):
            hot = (columns[:, stripe : stripe + 1] == lane_f).astype(jnp.bfloat16)
            keys_hot[t, stripe % 2, (stripe // 2) * 128 : (stripe // 2 + 1) * 128, :] = hot
        return 0

    lax.fori_loop(0, 4, key_columns, 0)

    def query_columns(a, _):
        columns = bucket_columns(block_at(row, a))
        for stripe in range(4):
            own = jnp.where(
                core == 0, columns[:, 2 * stripe : 2 * stripe + 1], columns[:, 2 * stripe + 1 : 2 * stripe + 2]
            )
            hot = (own == lane_f).astype(jnp.bfloat16)
            bias = lax.dot_general(hot, toeplitz, NT, preferred_element_type=jnp.float32)
            bias = bias.astype(jnp.bfloat16).reshape(2, 2, 32, NB)
            for half in range(2):
                q_wide[a, half, stripe * 64 : stripe * 64 + 64, NB:] = bias[:, half].reshape(64, NB)
        acc[a] = jnp.zeros((2, 256, 128), jnp.float32)
        return 0

    lax.fori_loop(0, 4, query_columns, 0)

    def unpack_queries(a):
        packed = q_packed[a].astype(jnp.float32)
        low = lax.broadcasted_iota(jnp.int32, (256, 128), 1) < DH
        q_wide[a, 0, :, :NB] = jnp.where(low, packed, 0.0).astype(jnp.bfloat16)
        q_wide[a, 1, :, :NB] = jnp.where(low, pltpu.roll(packed, DH, 1), 0.0).astype(jnp.bfloat16)

    def kv_copy(slot, d):
        return pltpu.make_async_remote_copy(
            src_ref=kv.at[slot, core],
            dst_ref=kv.at[slot, core],
            send_sem=kv_send.at[d - 1],
            recv_sem=kv_recv.at[d - 1],
            device_id=along_col(d),
            device_id_type=MESH,
        )

    def q_copy(slot, d):
        return pltpu.make_async_remote_copy(
            src_ref=q_packed.at[slot],
            dst_ref=q_packed.at[slot],
            send_sem=q_send.at[d - 1],
            recv_sem=q_recv.at[d - 1],
            device_id=along_row(d),
            device_id_type=MESH,
        )

    def twin_copy(slot, half, d):
        return pltpu.make_async_remote_copy(
            src_ref=kv.at[slot, half],
            dst_ref=kv.at[slot, half],
            send_sem=twin_send.at[d],
            recv_sem=twin_recv.at[d],
            device_id=twin,
            device_id_type=MESH,
        )

    def forward(i, _):
        source = lax.rem(z + 8 - away(i), 8)
        arrived_kv(source).wait_recv()
        piece = kv.at[row, core, pl.ds(pl.multiple_of(unit_offset(source) * 64, 64), 64)]
        for d in key_steps[1:3]:
            pltpu.make_async_remote_copy(
                src_ref=piece, dst_ref=piece, send_sem=kv_send.at[d - 1], recv_sem=kv_recv.at[d - 1],
                device_id=along_col(d), device_id_type=MESH,
            ).start()
        arrived_q(source).wait_recv()
        packed = q_packed.at[col, pl.ds(pl.multiple_of(unit_offset(source) * 32, 32), 32)]
        for d in (1, 3, 2):
            pltpu.make_async_remote_copy(
                src_ref=packed, dst_ref=packed, send_sem=q_send.at[d - 1], recv_sem=q_recv.at[d - 1],
                device_id=along_row(d), device_id_type=MESH,
            ).start()
        pltpu.make_async_remote_copy(
            src_ref=piece, dst_ref=piece, send_sem=twin_send.at[0], recv_sem=twin_recv.at[0],
            device_id=twin, device_id_type=MESH,
        ).start()
        return 0

    lax.fori_loop(0, 8, forward, 0, unroll=True)
    kv_copy(row, key_steps[3]).start()
    unpack_queries(col)

    def activate(halved):
        return (halved + halved * jnp.tanh(halved)).astype(jnp.bfloat16)

    def attend_diagonal(unit0, keys):
        rows = slice(unit0 * 32, unit0 * 32 + 128)
        held = jnp.concatenate([kv[row, 0, :keys], kv[row, 1, :keys]], axis=0)
        hot = jnp.concatenate([keys_hot[row, 0, :keys], keys_hot[row, 1, :keys]], axis=0)
        wide = jnp.concatenate([held, hot], axis=1)
        query = jnp.concatenate([q_wide[col, 0, rows], q_wide[col, 1, rows]], axis=0)
        scores = lax.dot_general(query, wide, NT, preferred_element_type=jnp.float32)
        place_q = lax.broadcasted_iota(jnp.int32, (256, 1), 0)
        unit = unit0 + (place_q % 128) // 32
        event_q = (unit // 2) * 256 + (unit % 2) * 64 + core * 128 + (place_q // 128) * 32 + place_q % 32
        place_k = lax.broadcasted_iota(jnp.int32, (1, 2 * keys), 1)
        event_k = ((place_k % keys) // 128) * 256 + (place_k // keys) * 128 + place_k % 128
        weights = jnp.where(event_k <= event_q, activate(scores), jnp.zeros((), jnp.bfloat16))
        total = jnp.dot(weights, held, preferred_element_type=jnp.float32)
        acc[col, 0, rows] += total[:128]
        acc[col, 1, rows] += total[128:]

    def attend(quarters, t, halves):
        held = kv[t].reshape(1024, 128)
        wide = jnp.concatenate([held, keys_hot[t].reshape(1024, 128)], axis=1)
        for quarter in quarters:
            a = mirrored(row, quarter)
            for half in halves:
                scores = lax.dot_general(q_wide[a, half], wide, NT, preferred_element_type=jnp.float32)
                acc[a, half] += jnp.dot(activate(scores), held, preferred_element_type=jnp.float32)

    def first_after(t):
        return mirrored(t, col) + jnp.where(row > t, 0, 1)

    def attend_all(t, halves, done=lambda quarter: None):
        first = first_after(t)
        odd = lax.rem(4 - first, 2)

        def two(k, _):
            quarter = 3 - 2 * k
            attend([quarter, quarter - 1], t, halves)
            done(quarter)
            done(quarter - 1)
            return 0

        lax.fori_loop(0, (4 - first) // 2, two, 0)

        @pl.when(odd == 1)
        def _():
            attend([first], t, halves)
            done(first)

    def key_member(n):
        return lax.rem(row - key_steps[n] + 4, 4)

    twin_copy(row, 1 - core, 0).wait_recv()
    attend_diagonal(0, 256)
    attend_diagonal(4, 512)

    def pass_on(d):
        t = lax.rem(row - d + 4, 4)
        kv_copy(t, d).wait_recv()
        twin_copy(t, core, d).start()

    def take_queries(d):
        a = lax.rem(col - d + 4, 4)
        q_copy(a, d).wait_recv()
        unpack_queries(a)

    def take_keys(d):
        twin_copy(lax.rem(row - d + 4, 4), 1 - core, d).wait_recv()

    low_units = lax.broadcasted_iota(jnp.int32, (8, 16, 128), 2) < DH

    def stays_back(a, unit):
        return jnp.logical_and(mirrored(row, a) == x, unit == unit_offset(z))

    def message(a, unit):
        return pl.ds(pl.multiple_of((a * 8 + unit) * 16, 16), 16)

    def send_quarter(half, quarter):
        a = mirrored(row, quarter)
        total = acc[a, half].reshape(8, 32, 128)
        total = jnp.where(low_units, pltpu.roll(total[:, :16], DH, 2), total[:, 16:]).astype(jnp.bfloat16)
        outgoing[half, pl.ds(pl.multiple_of(a * 128, 128), 128)] = total.reshape(128, 128)

        def send_back(i, _):
            owner_z = lax.rem(z + away(7 - i), 8)
            unit = unit_offset(owner_z)
            source = outgoing.at[half, message(a, unit)]
            place = returned.at[half, z, col]
            start_either(
                stays_back(a, unit),
                (source, place, back_recv.at[half]),
                lambda: pltpu.make_async_remote_copy(
                    src_ref=source,
                    dst_ref=place,
                    send_sem=back_send.at[half],
                    recv_sem=back_recv.at[half],
                    device_id=device_at(mirrored(row, a), row, owner_z, core),
                    device_id_type=MESH,
                ),
            )
            return 0

        lax.fori_loop(0, 8, send_back, 0, unroll=True)

    def release(low, high):
        for half in range(2):

            def one(quarter, _, half=half):
                send_quarter(half, quarter)
                return 0

            lax.fori_loop(low, high, one, 0)

    pass_on(key_steps[1])
    pass_on(key_steps[2])
    for d in (1, 3, 2):
        take_queries(d)
    attend_all(row, (0, 1))
    take_keys(key_steps[1])
    attend_all(key_member(1), (0, 1))
    last = first_after(key_member(3))
    settled = jnp.minimum(first_after(key_member(2)), last)
    release(0, settled)
    take_keys(key_steps[2])
    pass_on(key_steps[3])
    attend_all(key_member(2), (0, 1))
    release(settled, last)
    take_keys(key_steps[3])
    for half in range(2):
        attend_all(key_member(3), (half,), lambda quarter, half=half: send_quarter(half, quarter))

    def sent_first(i, _):
        @pl.when(jnp.logical_not(jnp.logical_and(stays, i == z)))
        def _():
            phase1_kv(i, z).wait_send()
            phase1_q(i, z).wait_send()

        return 0

    lax.fori_loop(0, 8, sent_first, 0)
    twin_copy(row, core, 0).wait_send()
    for d in range(1, 4):
        kv_copy(row, d).wait_send()
        q_copy(col, d).wait_send()
        twin_copy(lax.rem(row - d + 4, 4), core, d).wait_send()
    for load in loads[3:]:
        load.wait()

    low16 = lax.broadcasted_iota(jnp.int32, (16, 128), 1) < DH
    score_acc[...] = jnp.zeros_like(score_acc)

    def score_half(half):
        pltpu.make_async_copy(returned.at[half], returned.at[half], back_recv.at[half]).wait()
        sums = [
            jnp.sum(returned[half, h].astype(jnp.float32), axis=0).astype(jnp.bfloat16).astype(jnp.float32)
            for h in range(HEADS)
        ]
        parts = []
        for group in range(HEADS // 2):
            even, odd = sums[2 * group], sums[2 * group + 1]
            first = jnp.where(low16, even, pltpu.roll(odd, DH, 1))
            second = jnp.where(low16, pltpu.roll(even, DH, 1), odd)
            parts.append(jnp.concatenate([first, second], axis=0))
        restored = jnp.concatenate(parts, axis=1)
        centred = restored - jnp.mean(restored, axis=-1, keepdims=True)
        variance = jnp.mean(centred * centred, axis=-1, keepdims=True)
        normed = centred * lax.rsqrt(variance + NORM_EPS)
        gate = jnp.concatenate(
            [planes[group, pl.ds(half * 128, 32, stride=4), :] for group in range(HEADS // 2)], axis=1
        )
        gated = (normed * gate).astype(jnp.bfloat16)
        layer = jnp.dot(gated, out_weight[...], preferred_element_type=jnp.float32)
        layer = (layer + history[half * 32 : half * 32 + 32].astype(jnp.float32)).astype(jnp.bfloat16)
        layer_ref[half * 32 : half * 32 + 32] = layer
        halved_layer = layer.astype(jnp.float32) * 0.5
        for part in range(2):
            events = halved_layer[part * 16 : part * 16 + 16]
            rows = slice(half * 256 + part * 128, half * 256 + part * 128 + 128)
            spread = jnp.broadcast_to(events[:, None, :], (16, CANDS, events.shape[1])).reshape(128, -1)
            paired[rows] = (spread * candidates[rows].astype(jnp.float32)).astype(jnp.bfloat16)
        rows = slice(half * 256, half * 256 + 256)

        def score_tile(i, _):
            columns = pl.ds(pl.multiple_of(i * HID_TILE, HID_TILE), HID_TILE)
            halved = jnp.dot(paired[rows], hidden_weight[:, columns], preferred_element_type=jnp.float32)
            scored = (halved + halved * jnp.tanh(halved)) * score_weight[:, columns]
            total = score_acc[rows]
            for part in range(HID_TILE // 128):
                total += scored[:, part * 128 : part * 128 + 128]
            score_acc[rows] = total
            return 0

        lax.fori_loop(0, hidden_weight.shape[1] // HID_TILE, score_tile, 0)

    score_half(0)
    score_half(1)
    scores_ref[...] = jnp.transpose(jnp.sum(score_acc[...].reshape(UNIT, CANDS, 128), axis=-1))
    for half in range(2):
        left = outgoing.at[half, pl.ds(0, 31 * 16)]
        pltpu.make_async_copy(left, left, back_send.at[half]).wait()


def per_device(
    projected, history, buckets, time_table, out_weight, candidates, hidden_weight, score_weight
):
    width = projected.shape[2]
    dim = history.shape[1]
    hid = hidden_weight.shape[1]
    vmem = pl.BlockSpec(memory_space=pltpu.VMEM)
    hbm = pl.BlockSpec(memory_space=pl.ANY)
    dma = pltpu.SemaphoreType.DMA
    bf16, f32 = jnp.bfloat16, jnp.float32
    rows = UNIT * CANDS
    layer, scores = pl.pallas_call(
        layer_kernel,
        out_shape=(
            pltpu.VMEM((UNIT, dim), bf16),
            pltpu.VMEM((CANDS, UNIT), f32),
        ),
        in_specs=[hbm] * 8,
        out_specs=(vmem, vmem),
        scratch_shapes=[
            pltpu.VMEM((UNIT, 4, width), bf16),
            pltpu.VMEM((128, 128), jnp.int32),
            pltpu.VMEM((HEADS, NB), f32),
            pltpu.VMEM((width, dim), bf16),
            pltpu.VMEM((UNIT, dim), bf16),
            pltpu.VMEM((rows, dim), bf16),
            pltpu.VMEM((dim, hid), bf16),
            pltpu.VMEM((1, hid), f32),
            dma((8,)),
            pltpu.VMEM((HEADS // 2, UNIT * 4, 128), f32),
            pltpu.VMEM((HEADS, UNIT, 128), bf16),
            pltpu.VMEM((HEADS, UNIT // 2, 128), bf16),
            pltpu.VMEM((rows, dim), bf16),
            pltpu.VMEM((rows, 128), f32),
            pltpu.VMEM((4, 2, 512, 128), bf16),
            pltpu.VMEM((4, 2, 512, 128), bf16),
            pltpu.VMEM((4, 256, 128), bf16),
            pltpu.VMEM((4, 2, 256, 256), bf16),
            pltpu.VMEM((4, 2, 256, 128), f32),
            pltpu.VMEM((2, 512, 128), bf16),
            pltpu.VMEM((2, 8, 4, 16, 128), bf16),
            dma((2, 8)), dma((16,)), dma((3,)), dma((3,)), dma((3,)), dma((3,)),
            dma((4,)), dma((4,)), dma((2,)), dma((2,)),
        ],
        compiler_params=pltpu.CompilerParams(
            collective_id=0, has_side_effects=True, vmem_limit_bytes=56 << 20
        ),
        name="layer",
    )(
        projected, buckets.reshape(128, 128), time_table, out_weight, history,
        candidates.reshape(rows, dim), hidden_weight, score_weight.reshape(1, hid),
    )
    return layer, scores.T


def solution(mesh):
    rows = ("blk", "uly")
    return jax.shard_map(
        per_device,
        mesh=mesh,
        in_specs=(
            P(rows, None, None), P(rows, None), P(), P(), P(), P(rows, None, None), P(), P(),
        ),
        out_specs=(P(rows, None), P(rows, None)),
        check_vma=False,
    )
```

```python
import jax
import jax.numpy as jnp
from jax import lax
from jax.experimental import pallas as pl
from jax.experimental.pallas import tpu as pltpu
from jax.sharding import PartitionSpec as P

MESH = pl.DeviceIdType.MESH
NORM_EPS = 1e-05
DH = 64
CANDS = 8
UNIT = 64
HEADS = 8
HID_TILE = 4096
NB = 128
NT = (((1,), (1,)), ((), ()))


def device_at(x, y, z, core):
    return (x * 32 + y * 8 + lax.rem(z, 4) * 2 + core, z // 4)


def mirrored(row, col):
    return col + lax.rem(row, 2) * (3 - 2 * col)


def block_at(row, col):
    return 4 * mirrored(row, col) + row


def layer_kernel(
    projected_hbm, buckets_hbm, table_hbm, out_weight_hbm, history_hbm, candidates_hbm, hidden_hbm, score_hbm,
    layer_ref, scores_ref,
    projected, buckets_ref, table_ref, out_weight, history, candidates, hidden_weight, score_weight, load_sem,
    planes, kv_ref, q_ref, paired, score_acc,
    kv, keys_hot, q_packed, q_wide, acc, outgoing, returned,
    p1_send, p1_recv, kv_send, kv_recv, q_send, q_recv, twin_send, twin_recv, back_send, back_recv,
):
    blk, uly = lax.axis_index("blk"), lax.axis_index("uly")
    x, y = blk // 32, lax.rem(blk // 8, 4)
    z_lo, core = lax.rem(blk // 2, 4), lax.rem(blk, 2)
    z = uly * 4 + z_lo
    home_row, home_col = y, mirrored(y, x)
    target_x, target_y = home_col, home_row
    stays = y % 2 == 0
    row, col = y, x
    source_x, source_y = mirrored(row, col), row
    twin = device_at(x, y, z, 1 - core)

    early = mirrored(row, col) < 2
    key_steps = [
        jnp.int32(0), jnp.where(early, 2, 1), jnp.where(early, 1, 3), jnp.where(early, 3, 2),
    ]

    def along_col(d):
        return device_at(x, lax.rem(y + d, 4), z, core)

    def along_row(d):
        return device_at(lax.rem(x + d, 4), y, z, core)

    loads = [
        pltpu.make_async_copy(src, dst, load_sem.at[i])
        for i, (src, dst) in enumerate(
            (
                (projected_hbm, projected),
                (buckets_hbm, buckets_ref),
                (table_hbm, table_ref),
                (out_weight_hbm, out_weight),
                (history_hbm, history),
                (candidates_hbm, candidates),
                (score_hbm, score_weight),
                (hidden_hbm, hidden_weight),
            )
        )
    ]
    for load in loads[:3]:
        load.start()

    barrier = pltpu.get_barrier_semaphore()

    def greet(i, _):
        @pl.when(jnp.logical_not(jnp.logical_and(stays, i == z)))
        def _():
            pl.semaphore_signal(
                barrier, inc=1, device_id=device_at(source_x, source_y, i, core), device_id_type=MESH
            )

        return 0

    lax.fori_loop(0, 8, greet, 0, unroll=True)
    for d in range(1, 4):
        pl.semaphore_signal(barrier, inc=1, device_id=along_col(d), device_id_type=MESH)
        pl.semaphore_signal(barrier, inc=1, device_id=along_row(d), device_id_type=MESH)
    pl.semaphore_signal(barrier, inc=1, device_id=twin, device_id_type=MESH)

    low64 = lax.broadcasted_iota(jnp.int32, (UNIT, 128), 1) < DH
    low_half = lax.broadcasted_iota(jnp.int32, (UNIT // 2, 128), 1) < DH
    loads[0].wait()
    for group in range(HEADS // 2):
        lanes = slice(group * 128, group * 128 + 128)
        planes[group] = projected[:, :, lanes].astype(jnp.float32).reshape(UNIT * 4, 128)
        value, query, key = [planes[group, pl.ds(plane, UNIT, stride=4), :] for plane in (1, 2, 3)]
        kv_ref[2 * group] = jnp.where(low64, key, pltpu.roll(value, DH, 1)).astype(jnp.bfloat16)
        kv_ref[2 * group + 1] = jnp.where(low64, pltpu.roll(key, DH, 1), value).astype(jnp.bfloat16)
        early, late = query[:32] * 0.0625, query[32:] * 0.0625
        q_ref[2 * group] = jnp.where(low_half, early, pltpu.roll(late, DH, 1)).astype(jnp.bfloat16)
        q_ref[2 * group + 1] = jnp.where(low_half, pltpu.roll(early, DH, 1), late).astype(jnp.bfloat16)
    pl.semaphore_wait(barrier, 14 + lax.rem(y, 2))

    def unit_offset(zz):
        return lax.rem(zz, 4) * 2 + zz // 4

    def phase1_kv(head, src_z):
        return pltpu.make_async_remote_copy(
            src_ref=kv_ref.at[head],
            dst_ref=kv.at[home_row, core, pl.ds(pl.multiple_of(unit_offset(src_z) * 64, 64), 64)],
            send_sem=p1_send.at[0, head],
            recv_sem=p1_recv.at[src_z],
            device_id=device_at(target_x, target_y, head, core),
            device_id_type=MESH,
        )

    def phase1_q(head, src_z):
        return pltpu.make_async_remote_copy(
            src_ref=q_ref.at[head],
            dst_ref=q_packed.at[home_col, pl.ds(pl.multiple_of(unit_offset(src_z) * 32, 32), 32)],
            send_sem=p1_send.at[1, head],
            recv_sem=p1_recv.at[8 + src_z],
            device_id=device_at(target_x, target_y, head, core),
            device_id_type=MESH,
        )

    def arrived_kv(src_z):
        return pltpu.make_async_remote_copy(
            src_ref=kv_ref.at[0],
            dst_ref=kv.at[row, core, pl.ds(pl.multiple_of(unit_offset(src_z) * 64, 64), 64)],
            send_sem=p1_send.at[0, 0],
            recv_sem=p1_recv.at[src_z],
            device_id=device_at(source_x, source_y, src_z, core),
            device_id_type=MESH,
        )

    def arrived_q(src_z):
        return pltpu.make_async_remote_copy(
            src_ref=q_ref.at[0],
            dst_ref=q_packed.at[col, pl.ds(pl.multiple_of(unit_offset(src_z) * 32, 32), 32)],
            send_sem=p1_send.at[1, 0],
            recv_sem=p1_recv.at[8 + src_z],
            device_id=device_at(source_x, source_y, src_z, core),
            device_id_type=MESH,
        )

    def away(i):
        return lax.rem((i + 1) // 2 + lax.rem(i + 1, 2) * (8 - 2 * ((i + 1) // 2)) + 8, 8)

    def start_either(here, local, remote):
        @pl.when(here)
        def _():
            pltpu.make_async_copy(*local).start()

        @pl.when(jnp.logical_not(here))
        def _():
            remote().start()

    def send_first(i, _):
        head = lax.rem(z + away(i), 8)
        place = kv.at[home_row, core, pl.ds(pl.multiple_of(unit_offset(z) * 64, 64), 64)]
        start_either(
            jnp.logical_and(stays, head == z),
            (kv_ref.at[head], place, p1_recv.at[z]),
            lambda: phase1_kv(head, z),
        )
        place = q_packed.at[home_col, pl.ds(pl.multiple_of(unit_offset(z) * 32, 32), 32)]
        start_either(
            jnp.logical_and(stays, head == z),
            (q_ref.at[head], place, p1_recv.at[8 + z]),
            lambda: phase1_q(head, z),
        )
        return 0

    lax.fori_loop(0, 8, send_first, 0, unroll=True)
    for load in loads[3:]:
        load.start()
    for load in loads[1:3]:
        load.wait()

    lane = lax.broadcasted_iota(jnp.int32, (128, NB), 1)
    lane_f = lane.astype(jnp.float32)

    def bucket_columns(block):
        rows = buckets_ref[pl.ds(pl.multiple_of(block * 8, 8), 8), :]
        return jnp.transpose(rows.astype(jnp.float32))

    toeplitz = pltpu.roll(
        jnp.broadcast_to(table_ref[pl.ds(z, 1), :] * 0.5, (NB, NB)), 0, 1, stride=1, stride_axis=0
    ).astype(jnp.bfloat16)

    def key_columns(t, _):
        columns = bucket_columns(block_at(t, col))
        for stripe in range(8):
            hot = (columns[:, stripe : stripe + 1] == lane_f).astype(jnp.bfloat16)
            keys_hot[t, stripe % 2, (stripe // 2) * 128 : (stripe // 2 + 1) * 128, :] = hot
        return 0

    lax.fori_loop(0, 4, key_columns, 0)

    def query_columns(a, _):
        columns = bucket_columns(block_at(row, a))
        for stripe in range(4):
            own = jnp.where(
                core == 0, columns[:, 2 * stripe : 2 * stripe + 1], columns[:, 2 * stripe + 1 : 2 * stripe + 2]
            )
            hot = (own == lane_f).astype(jnp.bfloat16)
            bias = lax.dot_general(hot, toeplitz, NT, preferred_element_type=jnp.float32)
            bias = bias.astype(jnp.bfloat16).reshape(2, 2, 32, NB)
            for half in range(2):
                q_wide[a, half, stripe * 64 : stripe * 64 + 64, NB:] = bias[:, half].reshape(64, NB)
        acc[a] = jnp.zeros((2, 256, 128), jnp.float32)
        return 0

    lax.fori_loop(0, 4, query_columns, 0)

    def unpack_queries(a):
        packed = q_packed[a].astype(jnp.float32)
        low = lax.broadcasted_iota(jnp.int32, (256, 128), 1) < DH
        q_wide[a, 0, :, :NB] = jnp.where(low, packed, 0.0).astype(jnp.bfloat16)
        q_wide[a, 1, :, :NB] = jnp.where(low, pltpu.roll(packed, DH, 1), 0.0).astype(jnp.bfloat16)

    def kv_copy(slot, d):
        return pltpu.make_async_remote_copy(
            src_ref=kv.at[slot, core],
            dst_ref=kv.at[slot, core],
            send_sem=kv_send.at[d - 1],
            recv_sem=kv_recv.at[d - 1],
            device_id=along_col(d),
            device_id_type=MESH,
        )

    def q_copy(slot, d):
        return pltpu.make_async_remote_copy(
            src_ref=q_packed.at[slot],
            dst_ref=q_packed.at[slot],
            send_sem=q_send.at[d - 1],
            recv_sem=q_recv.at[d - 1],
            device_id=along_row(d),
            device_id_type=MESH,
        )

    def twin_copy(slot, half, d):
        return pltpu.make_async_remote_copy(
            src_ref=kv.at[slot, half],
            dst_ref=kv.at[slot, half],
            send_sem=twin_send.at[d],
            recv_sem=twin_recv.at[d],
            device_id=twin,
            device_id_type=MESH,
        )

    def forward(i, _):
        source = lax.rem(z + 8 - away(i), 8)
        arrived_kv(source).wait_recv()
        piece = kv.at[row, core, pl.ds(pl.multiple_of(unit_offset(source) * 64, 64), 64)]
        for d in key_steps[1:3]:
            pltpu.make_async_remote_copy(
                src_ref=piece, dst_ref=piece, send_sem=kv_send.at[d - 1], recv_sem=kv_recv.at[d - 1],
                device_id=along_col(d), device_id_type=MESH,
            ).start()
        arrived_q(source).wait_recv()
        packed = q_packed.at[col, pl.ds(pl.multiple_of(unit_offset(source) * 32, 32), 32)]
        for d in (1, 3, 2):
            pltpu.make_async_remote_copy(
                src_ref=packed, dst_ref=packed, send_sem=q_send.at[d - 1], recv_sem=q_recv.at[d - 1],
                device_id=along_row(d), device_id_type=MESH,
            ).start()
        pltpu.make_async_remote_copy(
            src_ref=piece, dst_ref=piece, send_sem=twin_send.at[0], recv_sem=twin_recv.at[0],
            device_id=twin, device_id_type=MESH,
        ).start()
        return 0

    lax.fori_loop(0, 8, forward, 0, unroll=True)
    kv_copy(row, key_steps[3]).start()
    unpack_queries(col)

    def activate(halved):
        return (halved + halved * jnp.tanh(halved)).astype(jnp.bfloat16)

    def attend_diagonal(unit0, keys):
        rows = slice(unit0 * 32, unit0 * 32 + 128)
        held = jnp.concatenate([kv[row, 0, :keys], kv[row, 1, :keys]], axis=0)
        hot = jnp.concatenate([keys_hot[row, 0, :keys], keys_hot[row, 1, :keys]], axis=0)
        wide = jnp.concatenate([held, hot], axis=1)
        query = jnp.concatenate([q_wide[col, 0, rows], q_wide[col, 1, rows]], axis=0)
        scores = lax.dot_general(query, wide, NT, preferred_element_type=jnp.float32)
        place_q = lax.broadcasted_iota(jnp.int32, (256, 1), 0)
        unit = unit0 + (place_q % 128) // 32
        event_q = (unit // 2) * 256 + (unit % 2) * 64 + core * 128 + (place_q // 128) * 32 + place_q % 32
        place_k = lax.broadcasted_iota(jnp.int32, (1, 2 * keys), 1)
        event_k = ((place_k % keys) // 128) * 256 + (place_k // keys) * 128 + place_k % 128
        weights = jnp.where(event_k <= event_q, activate(scores), jnp.zeros((), jnp.bfloat16))
        total = jnp.dot(weights, held, preferred_element_type=jnp.float32)
        acc[col, 0, rows] += total[:128]
        acc[col, 1, rows] += total[128:]

    def attend(quarters, t, halves):
        held = kv[t].reshape(1024, 128)
        wide = jnp.concatenate([held, keys_hot[t].reshape(1024, 128)], axis=1)
        for quarter in quarters:
            a = mirrored(row, quarter)
            for half in halves:
                scores = lax.dot_general(q_wide[a, half], wide, NT, preferred_element_type=jnp.float32)
                acc[a, half] += jnp.dot(activate(scores), held, preferred_element_type=jnp.float32)

    def first_after(t):
        return mirrored(t, col) + jnp.where(row > t, 0, 1)

    def attend_all(t, halves, done=lambda quarter: None):
        first = first_after(t)
        odd = lax.rem(4 - first, 2)

        def two(k, _):
            quarter = 3 - 2 * k
            attend([quarter, quarter - 1], t, halves)
            done(quarter)
            done(quarter - 1)
            return 0

        lax.fori_loop(0, (4 - first) // 2, two, 0)

        @pl.when(odd == 1)
        def _():
            attend([first], t, halves)
            done(first)

    def key_member(n):
        return lax.rem(row - key_steps[n] + 4, 4)

    twin_copy(row, 1 - core, 0).wait_recv()
    attend_diagonal(0, 256)
    attend_diagonal(4, 512)

    def pass_on(d):
        t = lax.rem(row - d + 4, 4)
        kv_copy(t, d).wait_recv()
        twin_copy(t, core, d).start()

    def take_queries(d):
        a = lax.rem(col - d + 4, 4)
        q_copy(a, d).wait_recv()
        unpack_queries(a)

    def take_keys(d):
        twin_copy(lax.rem(row - d + 4, 4), 1 - core, d).wait_recv()

    low_units = lax.broadcasted_iota(jnp.int32, (8, 16, 128), 2) < DH

    def stays_back(a, unit):
        return jnp.logical_and(mirrored(row, a) == x, unit == unit_offset(z))

    def message(a, unit):
        return pl.ds(pl.multiple_of((a * 8 + unit) * 16, 16), 16)

    def send_quarter(half, quarter):
        a = mirrored(row, quarter)
        total = acc[a, half].reshape(8, 32, 128)
        total = jnp.where(low_units, pltpu.roll(total[:, :16], DH, 2), total[:, 16:]).astype(jnp.bfloat16)
        outgoing[half, pl.ds(pl.multiple_of(a * 128, 128), 128)] = total.reshape(128, 128)

        def send_back(i, _):
            owner_z = lax.rem(z + away(7 - i), 8)
            unit = unit_offset(owner_z)
            source = outgoing.at[half, message(a, unit)]
            place = returned.at[half, z, col]
            start_either(
                stays_back(a, unit),
                (source, place, back_recv.at[half]),
                lambda: pltpu.make_async_remote_copy(
                    src_ref=source,
                    dst_ref=place,
                    send_sem=back_send.at[half],
                    recv_sem=back_recv.at[half],
                    device_id=device_at(mirrored(row, a), row, owner_z, core),
                    device_id_type=MESH,
                ),
            )
            return 0

        lax.fori_loop(0, 8, send_back, 0, unroll=True)

    def release(low, high):
        for half in range(2):

            def one(quarter, _, half=half):
                send_quarter(half, quarter)
                return 0

            lax.fori_loop(low, high, one, 0)

    pass_on(key_steps[1])
    pass_on(key_steps[2])
    for d in (1, 3, 2):
        take_queries(d)
    attend_all(row, (0, 1))
    take_keys(key_steps[1])
    attend_all(key_member(1), (0, 1))
    last = first_after(key_member(3))
    settled = jnp.minimum(first_after(key_member(2)), last)
    release(0, settled)
    take_keys(key_steps[2])
    pass_on(key_steps[3])
    attend_all(key_member(2), (0, 1))
    release(settled, last)
    take_keys(key_steps[3])
    for half in range(2):
        attend_all(key_member(3), (half,), lambda quarter, half=half: send_quarter(half, quarter))

    def sent_first(i, _):
        @pl.when(jnp.logical_not(jnp.logical_and(stays, i == z)))
        def _():
            phase1_kv(i, z).wait_send()
            phase1_q(i, z).wait_send()

        return 0

    lax.fori_loop(0, 8, sent_first, 0)
    twin_copy(row, core, 0).wait_send()
    for d in range(1, 4):
        kv_copy(row, d).wait_send()
        q_copy(col, d).wait_send()
        twin_copy(lax.rem(row - d + 4, 4), core, d).wait_send()
    for load in loads[3:]:
        load.wait()

    low16 = lax.broadcasted_iota(jnp.int32, (16, 128), 1) < DH
    score_acc[...] = jnp.zeros_like(score_acc)

    def score_half(half):
        pltpu.make_async_copy(returned.at[half], returned.at[half], back_recv.at[half]).wait()
        sums = [
            jnp.sum(returned[half, h].astype(jnp.float32), axis=0).astype(jnp.bfloat16).astype(jnp.float32)
            for h in range(HEADS)
        ]
        parts = []
        for group in range(HEADS // 2):
            even, odd = sums[2 * group], sums[2 * group + 1]
            first = jnp.where(low16, even, pltpu.roll(odd, DH, 1))
            second = jnp.where(low16, pltpu.roll(even, DH, 1), odd)
            parts.append(jnp.concatenate([first, second], axis=0))
        restored = jnp.concatenate(parts, axis=1)
        centred = restored - jnp.mean(restored, axis=-1, keepdims=True)
        variance = jnp.mean(centred * centred, axis=-1, keepdims=True)
        normed = centred * lax.rsqrt(variance + NORM_EPS)
        gate = jnp.concatenate(
            [planes[group, pl.ds(half * 128, 32, stride=4), :] for group in range(HEADS // 2)], axis=1
        )
        gated = (normed * gate).astype(jnp.bfloat16)
        layer = jnp.dot(gated, out_weight[...], preferred_element_type=jnp.float32)
        layer = (layer + history[half * 32 : half * 32 + 32].astype(jnp.float32)).astype(jnp.bfloat16)
        layer_ref[half * 32 : half * 32 + 32] = layer
        halved_layer = layer.astype(jnp.float32) * 0.5
        for part in range(2):
            events = halved_layer[part * 16 : part * 16 + 16]
            rows = slice(half * 256 + part * 128, half * 256 + part * 128 + 128)
            spread = jnp.broadcast_to(events[:, None, :], (16, CANDS, events.shape[1])).reshape(128, -1)
            paired[rows] = (spread * candidates[rows].astype(jnp.float32)).astype(jnp.bfloat16)
        rows = slice(half * 256, half * 256 + 256)

        def score_tile(i, _):
            columns = pl.ds(pl.multiple_of(i * HID_TILE, HID_TILE), HID_TILE)
            halved = jnp.dot(paired[rows], hidden_weight[:, columns], preferred_element_type=jnp.float32)
            scored = (halved + halved * jnp.tanh(halved)) * score_weight[:, columns]
            total = score_acc[rows]
            for part in range(HID_TILE // 128):
                total += scored[:, part * 128 : part * 128 + 128]
            score_acc[rows] = total
            return 0

        lax.fori_loop(0, hidden_weight.shape[1] // HID_TILE, score_tile, 0)

    score_half(0)
    score_half(1)
    scores_ref[...] = jnp.transpose(jnp.sum(score_acc[...].reshape(UNIT, CANDS, 128), axis=-1))
    for half in range(2):
        left = outgoing.at[half, pl.ds(0, 31 * 16)]
        pltpu.make_async_copy(left, left, back_send.at[half]).wait()


def per_device(
    projected, history, buckets, time_table, out_weight, candidates, hidden_weight, score_weight
):
    width = projected.shape[2]
    dim = history.shape[1]
    hid = hidden_weight.shape[1]
    vmem = pl.BlockSpec(memory_space=pltpu.VMEM)
    hbm = pl.BlockSpec(memory_space=pl.ANY)
    dma = pltpu.SemaphoreType.DMA
    bf16, f32 = jnp.bfloat16, jnp.float32
    rows = UNIT * CANDS
    layer, scores = pl.pallas_call(
        layer_kernel,
        out_shape=(
            pltpu.VMEM((UNIT, dim), bf16),
            pltpu.VMEM((CANDS, UNIT), f32),
        ),
        in_specs=[hbm] * 8,
        out_specs=(vmem, vmem),
        scratch_shapes=[
            pltpu.VMEM((UNIT, 4, width), bf16),
            pltpu.VMEM((128, 128), jnp.int32),
            pltpu.VMEM((HEADS, NB), f32),
            pltpu.VMEM((width, dim), bf16),
            pltpu.VMEM((UNIT, dim), bf16),
            pltpu.VMEM((rows, dim), bf16),
            pltpu.VMEM((dim, hid), bf16),
            pltpu.VMEM((1, hid), f32),
            dma((8,)),
            pltpu.VMEM((HEADS // 2, UNIT * 4, 128), f32),
            pltpu.VMEM((HEADS, UNIT, 128), bf16),
            pltpu.VMEM((HEADS, UNIT // 2, 128), bf16),
            pltpu.VMEM((rows, dim), bf16),
            pltpu.VMEM((rows, 128), f32),
            pltpu.VMEM((4, 2, 512, 128), bf16),
            pltpu.VMEM((4, 2, 512, 128), bf16),
            pltpu.VMEM((4, 256, 128), bf16),
            pltpu.VMEM((4, 2, 256, 256), bf16),
            pltpu.VMEM((4, 2, 256, 128), f32),
            pltpu.VMEM((2, 512, 128), bf16),
            pltpu.VMEM((2, 8, 4, 16, 128), bf16),
            dma((2, 8)), dma((16,)), dma((3,)), dma((3,)), dma((3,)), dma((3,)),
            dma((4,)), dma((4,)), dma((2,)), dma((2,)),
        ],
        compiler_params=pltpu.CompilerParams(
            collective_id=0, has_side_effects=True, vmem_limit_bytes=56 << 20
        ),
        name="layer",
    )(
        projected, buckets.reshape(128, 128), time_table, out_weight, history,
        candidates.reshape(rows, dim), hidden_weight, score_weight.reshape(1, hid),
    )
    return layer, scores.T


def solution(mesh):
    rows = ("blk", "uly")
    return jax.shard_map(
        per_device,
        mesh=mesh,
        in_specs=(
            P(rows, None, None), P(rows, None), P(), P(), P(), P(rows, None, None), P(), P(),
        ),
        out_specs=(P(rows, None), P(rows, None)),
        check_vma=False,
    )
```
